512 devices in a mesh: ctx: 32 (over z, core), head: 16 (over x, y).
Axes of the slice: x: 4, y: 4, z: 16, core: 2. Of those that a mesh axis runs over, the one named last changes fastest.
Arguments:
- queries: bfloat16 [12288, 2048], P(('ctx', 'head')), may hold values from -6 to 6
- keys: bfloat16 [12288, 2048], P(('ctx', 'head')), may hold values from -6 to 6
- values: bfloat16 [12288, 2048], P(('ctx', 'head')), may hold values from -6 to 6
- outputs: bfloat16 [12288, 2048], P(('ctx', 'head')), may hold values from -6 to 6
- grad_out: bfloat16 [12288, 2048], P(('ctx', 'head')), may hold values from -6 to 6
- log_sums: float32 [16, 12288], P('head', 'ctx')
- doc_ids: int32 [12288], P('ctx'), may hold values from 0 to 3, as said below
Outputs:
- grad_queries: bfloat16 [12288, 2048], P(('ctx', 'head'))
- grad_keys: bfloat16 [12288, 2048], P(('ctx', 'head'))
- grad_values: bfloat16 [12288, 2048], P(('ctx', 'head'))
The draws below stay inside these ranges and needn't reach their ends.
Inputs may be any that keep to these rules, and one draw needn't show every extreme that they name: `doc_ids`: document numbers never fall along the tokens; there are 4 documents, each of 1 to 6144 tokens, one of exactly 6144 tokens; document 0 starts at token 0.
All inputs are finite; a program needn't handle non-finite values.
Results may differ from the reference program's by a relative error of at most 0.017.
Values may be sent and summed in bfloat16 or wider, within the bound.
A program may use at most 128 MiB of HBM per device.

```python
import jax
import jax.numpy as jnp
import numpy as np
from jax import lax

DH = 128
TOK_DEV = 384
HEADS = 16
TOKENS = 12288
N_CTX = 32


def document_bounds(key):
    first_key, second_key = jax.random.split(key)
    leading = jax.random.randint(first_key, (), 1, TOKENS // 4)
    remainder = TOKENS // 2 - leading
    split_at = jax.random.randint(second_key, (), 1, remainder)
    positions = jnp.arange(TOKENS, dtype=jnp.int32)
    edges = jnp.stack([leading, leading + TOKENS // 2, leading + TOKENS // 2 + split_at]).astype(jnp.int32)
    doc_index = jnp.sum((positions[:, None] >= edges[None, :]).astype(jnp.int32), axis=1)
    doc_starts = jnp.where(doc_index == 0, 0, edges[jnp.maximum(doc_index - 1, 0)])
    visible = positions - doc_starts + 1 + jnp.where(doc_index > 0, leading, 0)
    return (doc_index, visible)


def draw_doc_ids(key, part):
    doc_index, visible = document_bounds(key)
    return doc_index


def draw_log_sums(key, part):
    doc_index, visible = document_bounds(key)
    key = jax.random.fold_in(key, 7)
    jitter = jax.random.uniform(key, (HEADS, TOKENS), jnp.float32, 0.3, 1.0)
    return jnp.log(visible.astype(jnp.float32))[None, :] + jitter


def block_levels(rng, dims, cuts, least, high):
    gain, own = 1.0, jax.random.fold_in(rng, 6)
    for axis_at, blocks in cuts:
        draws = jnp.exp(jax.random.uniform(jax.random.fold_in(own, axis_at), (blocks,), jnp.float32, least / len(cuts), high / len(cuts)))
        gain = gain * jnp.repeat(draws, dims[axis_at] // blocks).reshape([-1 if axis == axis_at else 1 for axis in range(len(dims))])
    return gain


def centred(rng, shape, deviation, most, pieces=(), held_as=jnp.bfloat16):
    gain = block_levels(rng, shape, pieces, -0.22, 0.18) if pieces else 1.0
    values = jax.random.normal(rng, shape, jnp.float32) * deviation * gain
    return jnp.minimum(jnp.maximum(values, -most), most).astype(held_as)


def setup_inputs(seed: int = 0) -> dict:
    streams_of = jax.random.split(jax.random.key(seed), 8)
    queries = centred(streams_of[0], (TOKENS, HEADS * DH), 1.0, 6.0, ((0, 512),))
    keys = centred(streams_of[1], (TOKENS, HEADS * DH), 1.0, 6.0, ((0, 512),))
    values = centred(streams_of[2], (TOKENS, HEADS * DH), 1.0, 6.0, ((0, 512),))
    outputs = centred(streams_of[3], (TOKENS, HEADS * DH), 1.0, 6.0, ((0, 512),))
    grad_out = centred(streams_of[4], (TOKENS, HEADS * DH), 1.0, 6.0, ((0, 512),))
    log_sums = draw_log_sums(jax.random.fold_in(streams_of[7], 71), 0)
    doc_ids = draw_doc_ids(jax.random.fold_in(streams_of[7], 71), 0)
    return {"queries": queries, "keys": keys, "values": values, "outputs": outputs, "grad_out": grad_out, "log_sums": log_sums, "doc_ids": doc_ids}


def tile_terms(query_tile, key_tile, value_tile, grad_tile, lse_rows, delta_rows, allowed):
    softmax_scale = key_tile.shape[1] ** -0.5
    scores = jnp.dot(query_tile, key_tile.T, preferred_element_type=jnp.float32) * softmax_scale
    probs = jnp.exp(jnp.where(allowed, scores - lse_rows[:, None], -1e30))
    dprobs = jnp.dot(grad_tile, value_tile.T, preferred_element_type=jnp.float32)
    dscores = (probs * (dprobs - delta_rows[:, None])).astype(jnp.bfloat16)
    return probs.astype(jnp.bfloat16), dscores


def contract_rows(left, right):
    return lax.dot_general(left, right, (((0,), (0,)), ((), ())), preferred_element_type=jnp.float32)


def head_grads(query_all, key_all, value_all, grad_all, lse_all, delta_all, doc_ids):
    tile_rows = TOK_DEV * min(max(1, 1024 // TOK_DEV), N_CTX)
    tile_count = TOKENS // tile_rows
    pair_table = np.array([(row_block, col_block) for row_block in range(tile_count) for col_block in range(row_block + 1)], dtype=np.int32)
    positions = jnp.arange(TOKENS, dtype=jnp.int32)
    empty = jnp.zeros((TOKENS, DH), jnp.float32)

    def step(carry, pair_entry):
        grad_q, grad_k, grad_v = carry
        row_first = (pair_entry[0] * tile_rows).astype(jnp.int32)
        col_first = (pair_entry[1] * tile_rows).astype(jnp.int32)
        query_tile = lax.dynamic_slice_in_dim(query_all, row_first, tile_rows, 0)
        grad_tile = lax.dynamic_slice_in_dim(grad_all, row_first, tile_rows, 0)
        key_tile = lax.dynamic_slice_in_dim(key_all, col_first, tile_rows, 0)
        value_tile = lax.dynamic_slice_in_dim(value_all, col_first, tile_rows, 0)
        lse_rows = lax.dynamic_slice_in_dim(lse_all, row_first, tile_rows, 0)
        delta_rows = lax.dynamic_slice_in_dim(delta_all, row_first, tile_rows, 0)
        row_pos = lax.dynamic_slice_in_dim(positions, row_first, tile_rows, 0)
        col_pos = lax.dynamic_slice_in_dim(positions, col_first, tile_rows, 0)
        row_docs = lax.dynamic_slice_in_dim(doc_ids, row_first, tile_rows, 0)
        col_docs = lax.dynamic_slice_in_dim(doc_ids, col_first, tile_rows, 0)
        allowed = (col_pos[None, :] <= row_pos[:, None]) & ((col_docs[None, :] == row_docs[:, None]) | (col_docs[None, :] == 0))
        probs, dscores = tile_terms(query_tile, key_tile, value_tile, grad_tile, lse_rows, delta_rows, allowed)
        old_rows = lax.dynamic_slice_in_dim(grad_q, row_first, tile_rows, 0)
        grad_q = lax.dynamic_update_slice_in_dim(grad_q, old_rows + jnp.dot(dscores, key_tile, preferred_element_type=jnp.float32), row_first, 0)
        old_keys = lax.dynamic_slice_in_dim(grad_k, col_first, tile_rows, 0)
        grad_k = lax.dynamic_update_slice_in_dim(grad_k, old_keys + contract_rows(dscores, query_tile), col_first, 0)
        old_vals = lax.dynamic_slice_in_dim(grad_v, col_first, tile_rows, 0)
        grad_v = lax.dynamic_update_slice_in_dim(grad_v, old_vals + contract_rows(probs, grad_tile), col_first, 0)
        return (grad_q, grad_k, grad_v), None

    (grad_q, grad_k, grad_v), _ = lax.scan(step, (empty, empty, empty), jnp.asarray(pair_table))
    softmax_scale = DH ** -0.5
    return grad_q * softmax_scale, grad_k * softmax_scale, grad_v


def reference(queries, keys, values, outputs, grad_out, log_sums, doc_ids):
    def by_head(matrix):
        return matrix.reshape(TOKENS, HEADS, DH).transpose(1, 0, 2)

    delta = jnp.sum(by_head(grad_out).astype(jnp.float32) * by_head(outputs).astype(jnp.float32), axis=2)

    def one_head(operands):
        return head_grads(operands[0], operands[1], operands[2], operands[3], operands[4], operands[5], doc_ids)

    grads = lax.map(one_head, (by_head(queries), by_head(keys), by_head(values), by_head(grad_out), log_sums, delta))

    def to_tokens(stacked):
        return stacked.transpose(1, 0, 2).reshape(TOKENS, HEADS * DH).astype(jnp.bfloat16)

    return to_tokens(grads[0]), to_tokens(grads[1]), to_tokens(grads[2])
```

```python
import jax
import jax.numpy as jnp
from jax import lax
from jax.experimental import pallas as pl
from jax.experimental.pallas import tpu as pltpu
from jax.sharding import PartitionSpec as P

DH = 128
NX, NY, NZ, NC = 4, 4, 16, 2
ROWS = 24
CTX_ROWS = NX * NY * ROWS
SPAN = NC * CTX_ROWS
Q_Z = NC * NY * ROWS
K_Z = NX * ROWS
Q_BLK = 2 * Q_Z
K_BLK = 2 * K_Z
N_BLK = NZ // 2
MESH = pl.DeviceIdType.MESH
F32 = jnp.float32
BF16 = jnp.bfloat16


def here():
    ctx, head = lax.axis_index("ctx"), lax.axis_index("head")
    return lax.div(head, NY), lax.rem(head, NY), lax.div(ctx, NC), lax.rem(ctx, NC)


def device(x, y, z, c):
    return (z * NC + c, x * NY + y)


def ring(me, step, size):
    away = lax.div(step, 2) + 1
    return lax.rem(jnp.where(lax.rem(step, 2) == 0, me + away, me - away + size), size)


def columns(head):
    return pl.ds(pl.multiple_of(head * DH, DH), DH)


def remote(src, dst, send, recv, to):
    return pltpu.make_async_remote_copy(
        src_ref=src, dst_ref=dst, send_sem=send, recv_sem=recv, device_id=to, device_id_type=MESH
    )


def loop(count, body):
    def step(i, carry):
        body(i)
        return carry

    lax.fori_loop(0, count, step, 0)


def gather_kernel(
    q, k, v, o, g, lse, doc,
    Q, K, V, G, L, D, C,
    delta,
    z_send, z_recv, own, d_send, d_recv, c_send, c_recv,
    hub_send, hub_recv, plane_send, plane_recv,
    x_send, x_recv, y_send, y_recv, s_send, s_recv,
):
    x, y, z, c = here()
    plane = x * NY + y
    sib = device(x, y, z, 1 - c)
    hub = z == plane
    zplane = lax.rem(z, NX * NY)
    hx, hy = lax.div(zplane, NY), lax.rem(zplane, NY)

    barrier = pltpu.get_barrier_semaphore()

    def greet(to):
        pl.semaphore_signal(barrier, inc=1, device_id=to, device_id_type=MESH)

    loop(NZ - 1, lambda i: greet(device(x, y, ring(z, i, NZ), c)))
    loop(NX - 1, lambda i: greet(device(ring(x, i, NX), y, z, c)))
    loop(NY - 1, lambda i: greet(device(x, ring(y, i, NY), z, c)))
    greet(sib)

    def plane_peer(i):
        other = lax.rem(plane + i + 1, NX * NY)
        return device(lax.div(other, NY), lax.rem(other, NY), z, c)

    @pl.when(hub)
    def _():
        loop(NX * NY - 1, lambda i: greet(plane_peer(i)))

    @pl.when(jnp.logical_not(hub))
    def _():
        greet(device(hx, hy, z, c))

    base = NZ - 1 + NX - 1 + NY - 1 + 1
    pl.semaphore_wait(barrier, base + jnp.where(hub, NX * NY - 1, 1))

    srcs = (k, v, q, g)

    def landing(a, zs):
        return (K.at[zs, x], V.at[zs, x], Q.at[zs, c, y], G.at[zs, c, y])[a]

    def z_copy(a, i):
        to = ring(z, i, NZ)
        return remote(
            srcs[a].at[:, columns(to)], landing(a, z), z_send.at[a, i], z_recv.at[a, z],
            device(x, y, to, c),
        )

    def own_copy(a):
        return pltpu.make_async_copy(srcs[a].at[:, columns(z)], landing(a, z), own.at[a])

    for a in range(4):
        own_copy(a).start()
        loop(NZ - 1, lambda i, a=a: z_copy(a, i).start())

    lse_own = pltpu.make_async_copy(lse, L.at[c, z], own.at[4])

    def lse_copy(to, frm):
        return remote(lse, L.at[c, z], hub_send, hub_recv.at[frm], device(x, y, to, c))

    @pl.when(hub)
    def _():
        lse_own.start()

    @pl.when(jnp.logical_not(hub))
    def _():
        lse_copy(plane, z).start()

    doc_own = pltpu.make_async_copy(doc, C.at[c, z], own.at[5])
    doc_own.start()

    def doc_copy(i, frm):
        return remote(doc, C.at[c, z], c_send.at[i], c_recv.at[frm], device(x, y, ring(z, i, NZ), c))

    loop(NZ - 1, lambda i: doc_copy(i, z).start())

    lane = lax.broadcasted_iota(jnp.int32, (ROWS, DH), 1)
    sums = jnp.zeros((ROWS, DH), F32)
    for h in range(NZ):
        cols = slice(h * DH, (h + 1) * DH)
        row = jnp.sum(g[:, cols].astype(F32) * o[:, cols].astype(F32), axis=1, keepdims=True)
        sums = jnp.where(lane == h, row, sums)
    turned = jnp.concatenate([sums, jnp.zeros((DH - ROWS, DH), F32)], axis=0).T
    for h in range(NZ):
        delta[h] = turned[h : h + 1, :]

    def delta_copy(i):
        to = ring(z, i, NZ)
        return remote(delta.at[to], D.at[z, c, y], d_send.at[i], d_recv.at[z], device(x, y, to, c))

    delta_own = pltpu.make_async_copy(delta.at[z], D.at[z, c, y], own.at[6])
    delta_own.start()
    loop(NZ - 1, lambda i: delta_copy(i).start())

    def z_wait(a):
        own_copy(a).wait()

        def one(i):
            frm = ring(z, i, NZ)
            remote(
                srcs[a].at[:, columns(frm)], landing(a, frm), z_send.at[a, i], z_recv.at[a, frm], sib
            ).wait_recv()

        loop(NZ - 1, one)

    def x_copy(a, i, frm, to):
        part = (K, V)[a].at[:, frm]
        return remote(part, part, x_send.at[a, i], x_recv.at[a, frm], device(to, y, z, c))

    for a in range(2):
        z_wait(a)
        for i in range(NX - 1):
            x_copy(a, i, x, ring(x, i, NX)).start()

    def plane_copy(i):
        return remote(L.at[c], L.at[c], plane_send.at[i], plane_recv, plane_peer(i))

    def sib_copy(part, slot):
        return remote(part, part, s_send.at[slot], s_recv.at[slot], sib)

    @pl.when(hub)
    def _():
        lse_own.wait()

        def one(i):
            frm = ring(z, i, NZ)
            remote(lse, L.at[c, frm], hub_send, hub_recv.at[frm], sib).wait_recv()

        loop(NZ - 1, one)
        loop(NX * NY - 1, lambda i: plane_copy(i).start())

    ys = (Q, G, D)

    def y_copy(a, i, frm, to):
        part = ys[a].at[:, c, frm]
        return remote(part, part, y_send.at[a, i], y_recv.at[a, frm], device(x, to, z, c))

    def sib_y(a, frm, core):
        return sib_copy(ys[a].at[:, core, frm], a * NY + frm)

    delta_own.wait()
    loop(
        NZ - 1,
        lambda i: remote(
            delta.at[z], D.at[ring(z, i, NZ), c, y], d_send.at[i], d_recv.at[ring(z, i, NZ)], sib
        ).wait_recv(),
    )
    for a in (2, 0, 1):
        if a < 2:
            z_wait(2 + a)
        for i in range(NY - 1):
            y_copy(a, i, y, ring(y, i, NY)).start()
        sib_y(a, y, c).start()

    doc_own.wait()
    loop(
        NZ - 1,
        lambda i: remote(doc, C.at[c, ring(z, i, NZ)], c_send.at[i], c_recv.at[ring(z, i, NZ)], sib).wait_recv(),
    )
    sib_copy(C.at[c], 3 * NY).start()

    @pl.when(jnp.logical_not(hub))
    def _():
        remote(L.at[c], L.at[c], plane_send.at[0], plane_recv, sib).wait_recv()

    sib_copy(L.at[c], 3 * NY + 1).start()

    for a in (2, 0, 1):
        for i in range(NY - 1):
            frm = ring(y, i, NY)
            y_copy(a, i, frm, y).wait_recv()
            sib_y(a, frm, c).start()

    for a in range(2):
        for i in range(NX - 1):
            x_copy(a, i, ring(x, i, NX), x).wait_recv()
    for a in range(3):
        for frm in range(NY):
            sib_y(a, frm, 1 - c).wait_recv()
    sib_copy(C.at[1 - c], 3 * NY).wait_recv()
    sib_copy(L.at[1 - c], 3 * NY + 1).wait_recv()

    for a in range(4):
        loop(NZ - 1, lambda i, a=a: z_copy(a, i).wait_send())
    loop(NZ - 1, lambda i: doc_copy(i, z).wait_send())
    loop(NZ - 1, lambda i: delta_copy(i).wait_send())

    @pl.when(jnp.logical_not(hub))
    def _():
        lse_copy(plane, z).wait_send()

    @pl.when(hub)
    def _():
        loop(NX * NY - 1, lambda i: plane_copy(i).wait_send())

    for a in range(2):
        for i in range(NX - 1):
            x_copy(a, i, x, ring(x, i, NX)).wait_send()
    for a in range(3):
        for i in range(NY - 1):
            y_copy(a, i, y, ring(y, i, NY)).wait_send()
        for frm in range(NY):
            sib_y(a, frm, c).wait_send()
    sib_copy(C.at[c], 3 * NY).wait_send()
    sib_copy(L.at[c], 3 * NY + 1).wait_send()


def gather_inputs(q, k, v, o, g, lse, doc):
    dma = pltpu.SemaphoreType.DMA
    vmem = pl.BlockSpec(memory_space=pltpu.VMEM)
    hbm = pl.BlockSpec(memory_space=pl.ANY)
    kv = jax.ShapeDtypeStruct((NZ, NX, ROWS, DH), BF16)
    qg = jax.ShapeDtypeStruct((NZ, NC, NY, ROWS, DH), BF16)
    return pl.pallas_call(
        gather_kernel,
        out_shape=(
            qg, kv, kv, qg,
            jax.ShapeDtypeStruct((NC, NZ, 1, CTX_ROWS), F32),
            jax.ShapeDtypeStruct((NZ, NC, NY, 1, DH), F32),
            jax.ShapeDtypeStruct((NC, NZ, 1, CTX_ROWS), jnp.int32),
        ),
        in_specs=[vmem] * 7,
        out_specs=(hbm,) * 7,
        scratch_shapes=[
            pltpu.VMEM((NZ, 1, DH), F32),
            dma((4, NZ - 1)), dma((4, NZ)), dma((7,)),
            dma((NZ - 1,)), dma((NZ,)), dma((NZ - 1,)), dma((NZ,)),
            dma, dma((NZ,)), dma((NX * NY - 1,)), dma,
            dma((2, NX - 1)), dma((2, NX)), dma((3, NY - 1)), dma((3, NY)),
            dma((3 * NY + 2,)), dma((3 * NY + 2,)),
        ],
        compiler_params=pltpu.CompilerParams(collective_id=0, has_side_effects=True),
        name="gather_inputs",
    )(q, k, v, o, g, lse, doc)


def contract_last(left, right):
    return lax.dot_general(left, right, (((1,), (1,)), ((), ())), preferred_element_type=F32)


def contract_first(left, right):
    return lax.dot_general(left, right, (((0,), (0,)), ((), ())), preferred_element_type=F32)


def tile_kernel(Q, K, V, G, L, D, C, dQ, dK, dV, ks, vs, lse_s, delta_s, acc_k, acc_v):
    x, y, z, c = here()
    docs = C[...]
    ends = [jnp.sum((docs < d).astype(jnp.int32)) for d in (1, 2, 3)]

    def doc_start(pos):
        start = jnp.where(pos >= ends[0], ends[0], 0)
        start = jnp.where(pos >= ends[1], ends[1], start)
        return jnp.where(pos >= ends[2], ends[2], start)

    acc_k[...] = jnp.zeros_like(acc_k)
    acc_v[...] = jnp.zeros_like(acc_v)

    def gather_keys(i, carry):
        at = pl.ds(pl.multiple_of(i * K_BLK, K_BLK), K_BLK)
        ks[at, :] = K[pl.ds(2 * i, 2)].astype(F32).reshape(K_BLK, DH).astype(BF16)
        vs[at, :] = V[pl.ds(2 * i, 2)].astype(F32).reshape(K_BLK, DH).astype(BF16)
        return carry

    lax.fori_loop(0, N_BLK, gather_keys, 0)

    part = NY * ROWS
    lses, deltas = [], []
    for core in range(NC):
        mine = jnp.concatenate([L[core, zz] for zz in range(NZ)], axis=0)
        picked = mine[:, :part]
        for xx in range(1, NX):
            picked = jnp.where(x == xx, mine[:, xx * part : (xx + 1) * part], picked)
        lses.append(picked)
        for yy in range(NY):
            rows = jnp.concatenate([D[zz, core, yy] for zz in range(NZ)], axis=0)
            deltas.append(rows[:, :ROWS])
    lses = jnp.concatenate(lses, axis=1)
    deltas = jnp.concatenate(deltas, axis=1)
    for j in range(N_BLK):
        lse_s[j] = jnp.concatenate([lses[2 * j : 2 * j + 1], lses[2 * j + 1 : 2 * j + 2]], axis=1)
        delta_s[j] = jnp.concatenate([deltas[2 * j : 2 * j + 1], deltas[2 * j + 1 : 2 * j + 2]], axis=1)

    q_at = lax.broadcasted_iota(jnp.int32, (1, Q_BLK), 1)
    q_in = lax.rem(q_at, Q_Z)
    q_base = (
        lax.div(q_at, Q_Z) * SPAN + lax.div(q_in, part) * CTX_ROWS + x * part + lax.rem(q_in, part)
    )
    k_at = lax.broadcasted_iota(jnp.int32, (K_BLK, 1), 0)
    k_in = lax.rem(k_at, K_Z)
    k_base = (
        lax.div(k_at, K_Z) * SPAN
        + c * CTX_ROWS
        + lax.div(k_in, ROWS) * part
        + y * ROWS
        + lax.rem(k_in, ROWS)
    )
    scale = DH**-0.5

    def query_block(j, carry):
        qb = Q[pl.ds(2 * j, 2)].astype(F32).reshape(Q_BLK, DH).astype(BF16)
        gb = G[pl.ds(2 * j, 2)].astype(F32).reshape(Q_BLK, DH).astype(BF16)
        q_pos = q_base + j * (2 * SPAN)
        start = doc_start(q_pos)
        lse, delta = lse_s[j], delta_s[j]

        def tile(i, causal):
            at = pl.ds(pl.multiple_of(i * K_BLK, K_BLK), K_BLK)
            kb, vb = ks[at, :], vs[at, :]
            k_pos = k_base + i * (2 * SPAN)
            key = jnp.where(k_pos < ends[0], NZ * SPAN, k_pos)
            allowed = key >= start
            if causal:
                allowed = allowed & (k_pos <= q_pos)
            s = contract_last(kb, qb) * scale - lse
            p = jnp.where(allowed, jnp.exp(s), 0.0)
            ds = (p * (contract_last(vb, gb) - delta)).astype(BF16)
            acc_v[at, :] += jnp.dot(p.astype(BF16), gb, preferred_element_type=F32)
            acc_k[at, :] += jnp.dot(ds, qb, preferred_element_type=F32)
            return contract_first(ds, kb)

        total = lax.fori_loop(
            0, j, lambda i, t: t + tile(i, False), jnp.zeros((Q_BLK, DH), F32)
        )
        total = total + tile(j, True)
        dQ[pl.ds(2 * j, 2)] = total.reshape(2, NC, NY, ROWS, DH).astype(BF16)
        return carry

    lax.fori_loop(0, N_BLK, query_block, 0)
    for zz in range(NZ):
        at = slice(zz * K_Z, (zz + 1) * K_Z)
        dK[zz] = acc_k[at, :].reshape(NX, ROWS, DH).astype(BF16)
        dV[zz] = acc_v[at, :].reshape(NX, ROWS, DH).astype(BF16)


def tile_grads(Q, K, V, G, L, D, C):
    vmem = pl.BlockSpec(memory_space=pltpu.VMEM)
    kv = jax.ShapeDtypeStruct((NZ, NX, ROWS, DH), BF16)
    qg = jax.ShapeDtypeStruct((NZ, NC, NY, ROWS, DH), BF16)
    return pl.pallas_call(
        tile_kernel,
        out_shape=(qg, kv, kv),
        in_specs=[vmem] * 7,
        out_specs=(vmem,) * 3,
        scratch_shapes=[
            pltpu.VMEM((NZ * K_Z, DH), BF16),
            pltpu.VMEM((NZ * K_Z, DH), BF16),
            pltpu.VMEM((N_BLK, 1, Q_BLK), F32),
            pltpu.VMEM((N_BLK, 1, Q_BLK), F32),
            pltpu.VMEM((NZ * K_Z, DH), F32),
            pltpu.VMEM((NZ * K_Z, DH), F32),
        ],
        compiler_params=pltpu.CompilerParams(vmem_limit_bytes=48 * 1024 * 1024),
        name="tile_grads",
    )(Q, K, V, G, L, D, C)


def return_kernel(
    dQ, dK, dV, oq, ok, ov, rq, rk, rv, res,
    q_send, q_recv, k_send, k_recv, own, z_send, z_recv,
):
    x, y, z, c = here()
    barrier = pltpu.get_barrier_semaphore()

    def greet(to):
        pl.semaphore_signal(barrier, inc=1, device_id=to, device_id_type=MESH)

    def q_peer(i):
        other = lax.rem(y * NC + c + i + 1, NY * NC)
        return lax.div(other, NC), lax.rem(other, NC)

    def q_dev(i):
        yy, cc = q_peer(i)
        return device(x, yy, z, cc)

    loop(NZ - 1, lambda i: greet(device(x, y, ring(z, i, NZ), c)))
    loop(NX - 1, lambda i: greet(device(ring(x, i, NX), y, z, c)))
    loop(NY * NC - 1, lambda i: greet(q_dev(i)))
    pl.semaphore_wait(barrier, NZ - 1 + NX - 1 + NY * NC - 1)

    pairs = ((dK, rk), (dV, rv))

    def k_copy(a, i, frm, to):
        src, dst = pairs[a]
        return remote(src.at[:, to], dst.at[frm], k_send.at[a, i], k_recv.at[a, frm], device(to, y, z, c))

    def q_copy(i, frm):
        yy, cc = q_peer(i)
        return remote(dQ.at[:, cc, yy], rq.at[frm], q_send.at[i], q_recv.at[frm], device(x, yy, z, cc))

    me = y * NC + c
    for a in range(2):
        for i in range(NX - 1):
            k_copy(a, i, x, ring(x, i, NX)).start()
    loop(NY * NC - 1, lambda i: q_copy(i, me).start())
    own_k = [pltpu.make_async_copy(pairs[a][0].at[:, x], pairs[a][1].at[x], own.at[a]) for a in range(2)]
    own_q = pltpu.make_async_copy(dQ.at[:, c, y], rq.at[me], own.at[2])
    for copy in (*own_k, own_q):
        copy.start()

    outs = (ok, ov, oq)

    def z_copy(a, i):
        to = ring(z, i, NZ)
        return remote(
            res.at[a, to], outs[a].at[:, columns(z)], z_send.at[a, i], z_recv.at[a, z],
            device(x, y, to, c),
        )

    def home(a):
        return pltpu.make_async_copy(res.at[a, z], outs[a].at[:, columns(z)], own.at[3 + a])

    def send_home(a):
        home(a).start()
        loop(NZ - 1, lambda i: z_copy(a, i).start())

    scale = DH**-0.5
    for a in range(2):
        for i in range(NX - 1):
            k_copy(a, i, ring(x, i, NX), x).wait_recv()
        own_k[a].wait()
        landed = pairs[a][1]

        def add_keys(zz, a=a, landed=landed):
            total = landed[0, zz].astype(F32)
            for xx in range(1, NX):
                total += landed[xx, zz].astype(F32)
            res[a, zz] = (total * scale if a == 0 else total).astype(BF16)

        loop(NZ, add_keys)
        send_home(a)

    loop(NY * NC - 1, lambda i: q_copy(i, lax.rem(me + i + 1, NY * NC)).wait_recv())
    own_q.wait()

    def add_queries(zz):
        total = rq[0, zz].astype(F32)
        for src in range(1, NY * NC):
            total += rq[src, zz].astype(F32)
        res[2, zz] = (total * scale).astype(BF16)

    loop(NZ, add_queries)
    send_home(2)

    for a in range(3):
        home(a).wait()

        def one(i, a=a):
            frm = ring(z, i, NZ)
            remote(
                res.at[a, frm], outs[a].at[:, columns(frm)], z_send.at[a, i], z_recv.at[a, frm],
                device(x, y, frm, c),
            ).wait_recv()

        loop(NZ - 1, one)

    for a in range(2):
        for i in range(NX - 1):
            k_copy(a, i, x, ring(x, i, NX)).wait_send()
    loop(NY * NC - 1, lambda i: q_copy(i, me).wait_send())
    for a in range(3):
        loop(NZ - 1, lambda i, a=a: z_copy(a, i).wait_send())


def return_grads(dQ, dK, dV):
    dma = pltpu.SemaphoreType.DMA
    hbm = pl.BlockSpec(memory_space=pl.ANY)
    out = jax.ShapeDtypeStruct((ROWS, NZ * DH), BF16)
    return pl.pallas_call(
        return_kernel,
        out_shape=(out, out, out),
        in_specs=[hbm] * 3,
        out_specs=(hbm,) * 3,
        scratch_shapes=[
            pltpu.VMEM((NY * NC, NZ, ROWS, DH), BF16),
            pltpu.VMEM((NX, NZ, ROWS, DH), BF16),
            pltpu.VMEM((NX, NZ, ROWS, DH), BF16),
            pltpu.VMEM((3, NZ, ROWS, DH), BF16),
            dma((NY * NC - 1,)), dma((NY * NC,)), dma((2, NX - 1)), dma((2, NX)), dma((6,)),
            dma((3, NZ - 1)), dma((3, NZ)),
        ],
        compiler_params=pltpu.CompilerParams(
            collective_id=1, has_side_effects=True, vmem_limit_bytes=32 * 1024 * 1024
        ),
        name="return_grads",
    )(dQ, dK, dV)


def per_device(queries, keys, values, outputs, grad_out, log_sums, doc_ids):
    landed = gather_inputs(
        queries, keys, values, outputs, grad_out, log_sums, doc_ids.reshape(1, CTX_ROWS)
    )
    return return_grads(*tile_grads(*landed))


def solution(mesh):
    tokens = P(("ctx", "head"), None)
    return jax.shard_map(
        per_device,
        mesh=mesh,
        in_specs=(tokens,) * 5 + (P("head", "ctx"), P("ctx")),
        out_specs=(tokens,) * 3,
        check_vma=False,
    )
```

```python
import jax
import jax.numpy as jnp
from jax import lax
from jax.experimental import pallas as pl
from jax.experimental.pallas import tpu as pltpu
from jax.sharding import PartitionSpec as P

DH = 128
NX, NY, NZ, NC = 4, 4, 16, 2
ROWS = 24
CTX_ROWS = NX * NY * ROWS
SPAN = NC * CTX_ROWS
Q_Z = NC * NY * ROWS
K_Z = NX * ROWS
BLK = 4
N_BLK = NZ // BLK
Q_BLK = BLK * Q_Z
K_BLK = BLK * K_Z
PART = NY * ROWS
MESH = pl.DeviceIdType.MESH
F32 = jnp.float32
BF16 = jnp.bfloat16


def here():
    ctx, head = lax.axis_index("ctx"), lax.axis_index("head")
    return lax.div(head, NY), lax.rem(head, NY), lax.div(ctx, NC), lax.rem(ctx, NC)


def device(x, y, z, c):
    return (z * NC + c, x * NY + y)


def ring(me, step, size):
    away = lax.div(step, 2) + 1
    return lax.rem(jnp.where(lax.rem(step, 2) == 0, me + away, me - away + size), size)


def columns(head):
    return pl.ds(pl.multiple_of(head * DH, DH), DH)


def remote(src, dst, send, recv, to):
    return pltpu.make_async_remote_copy(
        src_ref=src, dst_ref=dst, send_sem=send, recv_sem=recv, device_id=to, device_id_type=MESH
    )


def loop(count, body):
    def step(i, carry):
        body(i)
        return carry

    lax.fori_loop(0, count, step, 0)


def contract_last(left, right):
    return lax.dot_general(left, right, (((1,), (1,)), ((), ())), preferred_element_type=F32)


def block(i, size):
    return slice(i * size, (i + 1) * size)


def kernel(
    q, k, v, o, g, lse, doc,
    oq, ok, ov,
    Q, K, V, G, L, D, C, delta, docs,
    qs, ks, vs, gs, kt, probs, lse_s, delta_s,
    dq, dk, dv, rq, rk, rv, res,
    z_send, z_recv, own, d_send, d_recv, c_send, c_recv,
    hub_send, hub_recv, plane_send, plane_recv,
    x_send, x_recv, y_send, y_recv, s_send, s_recv,
    q_send, q_recv, k_send, k_recv, v_send, v_recv, h_send, h_recv,
):
    x, y, z, c = here()
    plane = x * NY + y
    sib = device(x, y, z, 1 - c)
    hub = z == plane
    scale = DH**-0.5

    barrier = pltpu.get_barrier_semaphore()

    def greet(to):
        pl.semaphore_signal(barrier, inc=1, device_id=to, device_id_type=MESH)

    def plane_peer(i):
        other = lax.rem(plane + i + 1, NX * NY)
        return device(lax.div(other, NY), lax.rem(other, NY), z, c)

    def q_peer(i):
        other = lax.rem(y * NC + c + i + 1, NY * NC)
        return lax.div(other, NC), lax.rem(other, NC)

    def q_dev(i):
        yy, cc = q_peer(i)
        return device(x, yy, z, cc)

    loop(NZ - 1, lambda i: greet(device(x, y, ring(z, i, NZ), c)))
    loop(NX - 1, lambda i: greet(device(ring(x, i, NX), y, z, c)))
    loop(NY * NC - 1, lambda i: greet(q_dev(i)))

    @pl.when(hub)
    def _():
        loop(NX * NY - 1, lambda i: greet(plane_peer(i)))

    @pl.when(jnp.logical_not(hub))
    def _():
        greet(device(lax.div(z, NY), lax.rem(z, NY), z, c))

    docs[...] = doc[...].reshape(1, CTX_ROWS)
    pl.semaphore_wait(
        barrier, NZ - 1 + NX - 1 + NY * NC - 1 + jnp.where(hub, NX * NY - 1, 1)
    )

    def doc_copy(i, frm):
        return remote(docs, C.at[c, frm], c_send.at[i], c_recv.at[frm], device(x, y, ring(z, i, NZ), c))

    def lse_copy(frm):
        return remote(lse, L.at[c, frm], hub_send, hub_recv.at[frm], device(x, y, plane, c))

    doc_own = pltpu.make_async_copy(docs, C.at[c, z], own.at[5])
    lse_own = pltpu.make_async_copy(lse, L.at[c, z], own.at[4])

    @pl.when(hub)
    def _():
        lse_own.start()

    @pl.when(jnp.logical_not(hub))
    def _():
        lse_copy(z).start()

    doc_own.start()
    loop(NZ - 1, lambda i: doc_copy(i, z).start())

    srcs = (q, k, g, v)

    def landing(a, zs):
        return (Q.at[zs, c, y], K.at[zs, x], G.at[zs, c, y], V.at[zs, x])[a]

    def z_copy(a, i):
        to = ring(z, i, NZ)
        return remote(
            srcs[a].at[:, columns(to)], landing(a, z), z_send.at[a, i], z_recv.at[a, z],
            device(x, y, to, c),
        )

    def own_copy(a):
        return pltpu.make_async_copy(srcs[a].at[:, columns(z)], landing(a, z), own.at[a])

    for a in range(4):
        own_copy(a).start()
        loop(NZ - 1, lambda i, a=a: z_copy(a, i).start())

    def z_wait(a):
        own_copy(a).wait()

        def one(i):
            frm = ring(z, i, NZ)
            remote(
                srcs[a].at[:, columns(frm)], landing(a, frm), z_send.at[a, i], z_recv.at[a, frm],
                device(x, y, frm, c),
            ).wait_recv()

        loop(NZ - 1, one)

    lane = lax.broadcasted_iota(jnp.int32, (ROWS, DH), 1)
    sums = jnp.zeros((ROWS, DH), F32)
    for h in range(NZ):
        cols = block(h, DH)
        row = jnp.sum(g[:, cols].astype(F32) * o[:, cols].astype(F32), axis=1, keepdims=True)
        sums = jnp.where(lane == h, row, sums)
    turned = jnp.concatenate([sums, jnp.zeros((DH - ROWS, DH), F32)], axis=0).T
    for h in range(NZ):
        delta[h] = turned[h : h + 1, :]

    def delta_copy(i, to, frm):
        return remote(
            delta.at[to], D.at[frm, c, y], d_send.at[i], d_recv.at[frm], device(x, y, ring(z, i, NZ), c)
        )

    delta_own = pltpu.make_async_copy(delta.at[z], D.at[z, c, y], own.at[6])
    delta_own.start()
    loop(NZ - 1, lambda i: delta_copy(i, ring(z, i, NZ), z).start())

    def sib_copy(part, slot):
        return remote(part, part, s_send.at[slot], s_recv.at[slot], sib)

    ys = (Q, G, D)

    def y_copy(a, i, frm, to):
        part = ys[a].at[:, c, frm]
        return remote(part, part, y_send.at[a, i], y_recv.at[a, frm], device(x, to, z, c))

    def sib_y(a, frm, core):
        return sib_copy(ys[a].at[:, core, frm], a * NY + frm)

    def y_start(a):
        for i in range(NY - 1):
            y_copy(a, i, y, ring(y, i, NY)).start()
        sib_y(a, y, c).start()

    def y_relay(a):
        for i in range(NY - 1):
            frm = ring(y, i, NY)
            y_copy(a, i, frm, y).wait_recv()
            sib_y(a, frm, c).start()

    def y_wait(a):
        for frm in range(NY):
            sib_y(a, frm, 1 - c).wait_recv()

    def x_copy(a, i, frm, to):
        part = (K, V)[a].at[:, frm]
        return remote(part, part, x_send.at[a, i], x_recv.at[a, frm], device(to, y, z, c))

    def x_start(a):
        for i in range(NX - 1):
            x_copy(a, i, x, ring(x, i, NX)).start()

    def x_wait(a):
        for i in range(NX - 1):
            x_copy(a, i, ring(x, i, NX), x).wait_recv()

    def plane_copy(i):
        return remote(L.at[c], L.at[c], plane_send.at[i], plane_recv, plane_peer(i))

    def doc_sib(core):
        return sib_copy(C.at[core], 3 * NY)

    def lse_sib(core):
        return sib_copy(L.at[core], 3 * NY + 1)

    @pl.when(hub)
    def _():
        lse_own.wait()

        def one(i):
            lse_copy(ring(z, i, NZ)).wait_recv()

        loop(NZ - 1, one)
        loop(NX * NY - 1, lambda i: plane_copy(i).start())

    doc_own.wait()
    loop(NZ - 1, lambda i: doc_copy(i, ring(z, i, NZ)).wait_recv())
    doc_sib(c).start()

    z_wait(0)
    y_start(0)

    @pl.when(jnp.logical_not(hub))
    def _():
        plane_copy(0).wait_recv()

    lse_sib(c).start()
    z_wait(1)
    x_start(0)
    y_relay(0)
    lse_sib(1 - c).wait_recv()
    doc_sib(1 - c).wait_recv()
    ends = [jnp.sum((C[...] < d).astype(jnp.int32)) for d in (1, 2, 3)]

    def doc_start(pos):
        start = jnp.where(pos >= ends[0], ends[0], 0)
        start = jnp.where(pos >= ends[1], ends[1], start)
        return jnp.where(pos >= ends[2], ends[2], start)

    def lay_rows(by_plane, out):
        for j in range(N_BLK):
            out[j] = jnp.concatenate([by_plane[zz : zz + 1] for zz in range(BLK * j, BLK * (j + 1))], axis=1)

    parts = []
    for core in range(NC):
        mine = jnp.concatenate([L[core, zz] for zz in range(NZ)], axis=0)
        picked = mine[:, :PART]
        for xx in range(1, NX):
            picked = jnp.where(x == xx, mine[:, block(xx, PART)], picked)
        parts.append(picked)
    lay_rows(jnp.concatenate(parts, axis=1), lse_s)

    q_at = lax.broadcasted_iota(jnp.int32, (1, Q_BLK), 1)
    q_in = lax.rem(q_at, Q_Z)
    q_base = (
        lax.div(q_at, Q_Z) * SPAN + lax.div(q_in, PART) * CTX_ROWS + x * PART + lax.rem(q_in, PART)
    )
    k_at = lax.broadcasted_iota(jnp.int32, (K_BLK, 1), 0)
    k_in = lax.rem(k_at, K_Z)
    k_base = (
        lax.div(k_at, K_Z) * SPAN
        + c * CTX_ROWS
        + lax.div(k_in, ROWS) * PART
        + y * ROWS
        + lax.rem(k_in, ROWS)
    )

    def flat(src, out, rows):
        def step(zz):
            at = pl.ds(pl.multiple_of(zz * rows, rows), rows)
            out[at, :] = src[zz].astype(F32).reshape(rows, DH).astype(BF16)

        loop(NZ, step)

    z_wait(2)
    y_start(1)
    y_wait(0)
    flat(Q, qs, Q_Z)
    x_wait(0)
    flat(K, ks, K_Z)

    def probs_block(j):
        q_pos = q_base + j * (BLK * SPAN)
        start = doc_start(q_pos)
        for i in range(j + 1):
            k_pos = k_base + i * (BLK * SPAN)
            allowed = jnp.where(k_pos < ends[0], NZ * SPAN, k_pos) >= start
            if i == j:
                allowed = allowed & (k_pos <= q_pos)
            s = contract_last(ks[block(i, K_BLK), :], qs[block(j, Q_BLK), :])
            p = jnp.where(allowed, jnp.exp(s * scale - lse_s[j]), 0.0)
            probs[block(i, K_BLK), block(j, Q_BLK)] = p.astype(BF16)

    probs_block(0)
    probs_block(1)
    z_wait(3)
    x_start(1)
    y_relay(1)
    probs_block(2)
    probs_block(3)

    y_wait(1)
    flat(G, gs, Q_Z)

    def v_copy(i, frm, to):
        return remote(dv.at[:, to], rv.at[frm], v_send.at[i], v_recv.at[frm], device(to, y, z, c))

    for i in range(N_BLK):
        total = jnp.dot(
            probs[block(i, K_BLK), i * Q_BLK :], gs[i * Q_BLK :, :], preferred_element_type=F32
        )
        dv[BLK * i : BLK * (i + 1)] = total.reshape(BLK, NX, ROWS, DH).astype(BF16)
    for i in range(NX - 1):
        v_copy(i, x, ring(x, i, NX)).start()

    delta_own.wait()
    loop(NZ - 1, lambda i: delta_copy(i, z, ring(z, i, NZ)).wait_recv())
    y_start(2)
    y_relay(2)
    for i in range(N_BLK):
        kt[i] = ks[block(i, K_BLK), :].T
    y_wait(2)
    parts = []
    for core in range(NC):
        for yy in range(NY):
            rows = jnp.concatenate([D[zz, core, yy] for zz in range(NZ)], axis=0)
            parts.append(rows[:, :ROWS])
    lay_rows(jnp.concatenate(parts, axis=1), delta_s)
    x_wait(1)
    flat(V, vs, K_Z)

    me = y * NC + c

    def k_copy(j, i, frm, to):
        rows = pl.ds(BLK * j, BLK)
        return remote(
            dk.at[rows, to], rk.at[frm, rows], k_send.at[j, i], k_recv.at[j, frm], device(to, y, z, c)
        )

    def q_copy(j, i, frm):
        rows = pl.ds(BLK * j, BLK)
        yy, cc = q_peer(i)
        return remote(
            dq.at[rows, cc, yy], rq.at[frm, rows], q_send.at[j, i], q_recv.at[j, frm],
            device(x, yy, z, cc),
        )

    def grads_block(j):
        total = jnp.zeros((DH, Q_BLK), F32)
        for i in range(j + 1):
            dp = contract_last(vs[block(i, K_BLK), :], gs[block(j, Q_BLK), :])
            p = probs[block(i, K_BLK), block(j, Q_BLK)].astype(F32)
            ds = (p * (dp - delta_s[j])).astype(BF16)
            probs[block(i, K_BLK), block(j, Q_BLK)] = ds
            total += jnp.dot(kt[i], ds, preferred_element_type=F32)
        dq[BLK * j : BLK * (j + 1)] = total.T.reshape(BLK, NC, NY, ROWS, DH).astype(BF16)
        loop(NY * NC - 1, lambda i: q_copy(j, i, me).start())
        total = jnp.dot(
            probs[block(j, K_BLK), j * Q_BLK :], qs[j * Q_BLK :, :], preferred_element_type=F32
        )
        dk[BLK * j : BLK * (j + 1)] = total.reshape(BLK, NX, ROWS, DH).astype(BF16)
        for i in range(NX - 1):
            k_copy(j, i, x, ring(x, i, NX)).start()

    outs = (oq, ok, ov)

    def home_copy(a, to, frm):
        return remote(
            res.at[a, to], outs[a].at[:, columns(frm)], h_send.at[a, to], h_recv.at[a, frm],
            device(x, y, to, c),
        )

    def home_own(a):
        return pltpu.make_async_copy(res.at[a, z], outs[a].at[:, columns(z)], own.at[7 + a])

    def send_home(a, to):
        @pl.when(to == z)
        def _():
            home_own(a).start()

        @pl.when(to != z)
        def _():
            home_copy(a, to, z).start()

    def add_v():
        for i in range(NX - 1):
            v_copy(i, ring(x, i, NX), x).wait_recv()

        def one(zz):
            total = dv[zz, x].astype(F32)
            for i in range(NX - 1):
                total += rv[ring(x, i, NX), zz].astype(F32)
            res[2, zz] = total.astype(BF16)

        loop(NZ, one)
        loop(NZ, lambda i: send_home(2, lax.rem(z + i, NZ)))

    def add_block(j):
        for i in range(NX - 1):
            k_copy(j, i, ring(x, i, NX), x).wait_recv()
        loop(NY * NC - 1, lambda i: q_copy(j, i, lax.rem(me + i + 1, NY * NC)).wait_recv())

        def one(step):
            zz = BLK * j + step
            total = dk[zz, x].astype(F32)
            for i in range(NX - 1):
                total += rk[ring(x, i, NX), zz].astype(F32)
            res[1, zz] = (total * scale).astype(BF16)
            total = dq[zz, c, y].astype(F32)
            for i in range(NY * NC - 1):
                total += rq[lax.rem(me + i + 1, NY * NC), zz].astype(F32)
            res[0, zz] = (total * scale).astype(BF16)
            send_home(1, zz)
            send_home(0, zz)

        loop(BLK, one)

    grads_block(3)
    add_v()
    grads_block(2)
    add_block(3)
    grads_block(1)
    add_block(2)
    grads_block(0)
    add_block(1)
    add_block(0)

    for a in range(4):
        loop(NZ - 1, lambda i, a=a: z_copy(a, i).wait_send())
    loop(NZ - 1, lambda i: doc_copy(i, z).wait_send())
    loop(NZ - 1, lambda i: delta_copy(i, ring(z, i, NZ), z).wait_send())

    @pl.when(jnp.logical_not(hub))
    def _():
        lse_copy(z).wait_send()

    @pl.when(hub)
    def _():
        loop(NX * NY - 1, lambda i: plane_copy(i).wait_send())

    for a in range(2):
        for i in range(NX - 1):
            x_copy(a, i, x, ring(x, i, NX)).wait_send()
    for a in range(3):
        for i in range(NY - 1):
            y_copy(a, i, y, ring(y, i, NY)).wait_send()
        for frm in range(NY):
            sib_y(a, frm, c).wait_send()
    doc_sib(c).wait_send()
    lse_sib(c).wait_send()
    for i in range(NX - 1):
        v_copy(i, x, ring(x, i, NX)).wait_send()
    for j in range(N_BLK):
        for i in range(NX - 1):
            k_copy(j, i, x, ring(x, i, NX)).wait_send()
        loop(NY * NC - 1, lambda i, j=j: q_copy(j, i, me).wait_send())
    for a in range(3):
        home_own(a).wait()

        def one(i, a=a):
            peer = ring(z, i, NZ)
            home_copy(a, peer, z).wait_send()
            home_copy(a, z, peer).wait_recv()

        loop(NZ - 1, one)


def per_device(queries, keys, values, outputs, grad_out, log_sums, doc_ids):
    dma = pltpu.SemaphoreType.DMA
    vmem = pl.BlockSpec(memory_space=pltpu.VMEM)
    hbm = pl.BlockSpec(memory_space=pl.ANY)
    out = jax.ShapeDtypeStruct((ROWS, NZ * DH), BF16)
    kv, qg = (NZ, NX, ROWS, DH), (NZ, NC, NY, ROWS, DH)
    return pl.pallas_call(
        kernel,
        out_shape=(out, out, out),
        in_specs=[vmem] * 7,
        out_specs=(hbm,) * 3,
        scratch_shapes=[
            pltpu.VMEM(qg, BF16), pltpu.VMEM(kv, BF16), pltpu.VMEM(kv, BF16), pltpu.VMEM(qg, BF16),
            pltpu.VMEM((NC, NZ, 1, CTX_ROWS), F32),
            pltpu.VMEM((NZ, NC, NY, 1, DH), F32),
            pltpu.VMEM((NC, NZ, 1, CTX_ROWS), jnp.int32),
            pltpu.VMEM((NZ, 1, DH), F32), pltpu.VMEM((1, CTX_ROWS), jnp.int32),
            pltpu.VMEM((NZ * Q_Z, DH), BF16), pltpu.VMEM((NZ * K_Z, DH), BF16),
            pltpu.VMEM((NZ * K_Z, DH), BF16), pltpu.VMEM((NZ * Q_Z, DH), BF16),
            pltpu.VMEM((N_BLK, DH, K_BLK), BF16), pltpu.VMEM((NZ * K_Z, NZ * Q_Z), BF16),
            pltpu.VMEM((N_BLK, 1, Q_BLK), F32), pltpu.VMEM((N_BLK, 1, Q_BLK), F32),
            pltpu.VMEM(qg, BF16), pltpu.VMEM(kv, BF16), pltpu.VMEM(kv, BF16),
            pltpu.VMEM((NY * NC, NZ, ROWS, DH), BF16),
            pltpu.VMEM((NX, NZ, ROWS, DH), BF16), pltpu.VMEM((NX, NZ, ROWS, DH), BF16),
            pltpu.VMEM((3, NZ, ROWS, DH), BF16),
            dma((4, NZ - 1)), dma((4, NZ)), dma((10,)),
            dma((NZ - 1,)), dma((NZ,)), dma((NZ - 1,)), dma((NZ,)),
            dma, dma((NZ,)), dma((NX * NY - 1,)), dma,
            dma((2, NX - 1)), dma((2, NX)), dma((3, NY - 1)), dma((3, NY)),
            dma((3 * NY + 2,)), dma((3 * NY + 2,)),
            dma((N_BLK, NY * NC - 1)), dma((N_BLK, NY * NC)), dma((N_BLK, NX - 1)), dma((N_BLK, NX)),
            dma((NX - 1,)), dma((NX,)), dma((3, NZ)), dma((3, NZ)),
        ],
        compiler_params=pltpu.CompilerParams(
            collective_id=0, has_side_effects=True, vmem_limit_bytes=50 * 1024 * 1024
        ),
        name="attention_grads",
    )(queries, keys, values, outputs, grad_out, log_sums, doc_ids)


def solution(mesh):
    tokens = P(("ctx", "head"), None)
    return jax.shard_map(
        per_device,
        mesh=mesh,
        in_specs=(tokens,) * 5 + (P("head", "ctx"), P("ctx")),
        out_specs=(tokens,) * 3,
        check_vma=False,
    )
```

```python
import jax
import jax.numpy as jnp
from jax import lax
from jax.experimental import pallas as pl
from jax.experimental.pallas import tpu as pltpu
from jax.sharding import PartitionSpec as P

DH = 128
NX, NY, NZ, NC = 4, 4, 16, 2
ROWS = 24
CTX_ROWS = NX * NY * ROWS
SPAN = NC * CTX_ROWS
Q_Z = NC * NY * ROWS
K_Z = NX * ROWS
BLK = 4
N_BLK = NZ // BLK
Q_BLK = BLK * Q_Z
K_BLK = BLK * K_Z
PART = NY * ROWS
STATS = CTX_ROWS + DH
MESH = pl.DeviceIdType.MESH
F32 = jnp.float32
BF16 = jnp.bfloat16


def here():
    ctx, head = lax.axis_index("ctx"), lax.axis_index("head")
    return lax.div(head, NY), lax.rem(head, NY), lax.div(ctx, NC), lax.rem(ctx, NC)


def device(x, y, z, c):
    return (z * NC + c, x * NY + y)


def ring(me, step, size):
    away = lax.div(step, 2) + 1
    return lax.rem(jnp.where(lax.rem(step, 2) == 0, me + away, me - away + size), size)


def columns(head):
    return pl.ds(pl.multiple_of(head * DH, DH), DH)


def remote(src, dst, send, recv, to):
    return pltpu.make_async_remote_copy(
        src_ref=src, dst_ref=dst, send_sem=send, recv_sem=recv, device_id=to, device_id_type=MESH
    )


def loop(count, body):
    def step(i, carry):
        body(i)
        return carry

    lax.fori_loop(0, count, step, 0)


def contract_last(left, right):
    return lax.dot_general(left, right, (((1,), (1,)), ((), ())), preferred_element_type=F32)


def block(i, size):
    return slice(i * size, (i + 1) * size)


def kernel(
    q, k, v, o, g, lse, doc,
    oq, ok, ov,
    Q, K, V, G, L, D, delta, stats, doc_in, lse_in, g_in, o_in,
    qs, ks, vs, gs, kt, probs, lse_s, delta_s,
    dq, dk, dv, pq, rs, rq, rk, rv, res,
    z_send, z_recv, own, d_send, d_recv,
    hub_send, hub_recv, plane_send, plane_recv,
    x_send, x_recv, y_send, y_recv, s_send, s_recv,
    xv_send, xv_recv, p_send, p_recv,
    q_send, q_recv, k_send, k_recv, v_send, v_recv, h_send, h_recv,
):
    x, y, z, c = here()
    plane = x * NY + y
    sib = device(x, y, z, 1 - c)
    hub = z == plane
    scale = DH**-0.5

    barrier = pltpu.get_barrier_semaphore()

    def greet(to):
        pl.semaphore_signal(barrier, inc=1, device_id=to, device_id_type=MESH)

    def plane_peer(i):
        other = lax.rem(plane + i + 1, NX * NY)
        return device(lax.div(other, NY), lax.rem(other, NY), z, c)

    loop(NZ - 1, lambda i: greet(device(x, y, ring(z, i, NZ), c)))
    fetch = [
        pltpu.make_async_copy(src, dst, own.at[10 + i])
        for i, (src, dst) in enumerate(((doc, doc_in), (lse, lse_in), (g, g_in), (o, o_in)))
    ]
    for copy in fetch:
        copy.start()
    loop(NX - 1, lambda i: greet(device(ring(x, i, NX), y, z, c)))
    loop(NY - 1, lambda i: greet(device(x, ring(y, i, NY), z, c)))
    greet(sib)

    @pl.when(hub)
    def _():
        loop(NX * NY - 1, lambda i: greet(plane_peer(i)))

    @pl.when(jnp.logical_not(hub))
    def _():
        greet(device(lax.div(z, NY), lax.rem(z, NY), z, c))

    pl.semaphore_wait(
        barrier, NZ - 1 + NX - 1 + NY - 1 + 1 + jnp.where(hub, NX * NY - 1, 1)
    )

    def lse_copy(frm):
        return remote(stats, L.at[c, frm], hub_send, hub_recv.at[frm], device(x, y, plane, c))

    lse_own = pltpu.make_async_copy(stats, L.at[c, z], own.at[4])

    srcs = (q, k, g, v)

    def landing(a, zs):
        return (Q.at[zs, c, y], K.at[zs, x], G.at[zs, c, y], V.at[zs, x])[a]

    def z_copy(a, i):
        to = ring(z, i, NZ)
        return remote(
            srcs[a].at[:, columns(to)], landing(a, z), z_send.at[a, i], z_recv.at[a, z],
            device(x, y, to, c),
        )

    def own_copy(a):
        return pltpu.make_async_copy(srcs[a].at[:, columns(z)], landing(a, z), own.at[a])

    def z_start(a):
        own_copy(a).start()
        loop(NZ - 1, lambda i: z_copy(a, i).start())

    def z_wait_from(a, i):
        frm = ring(z, i, NZ)
        remote(
            srcs[a].at[:, columns(frm)], landing(a, frm), z_send.at[a, i], z_recv.at[a, frm],
            device(x, y, frm, c),
        ).wait_recv()

    def z_wait(a):
        own_copy(a).wait()
        loop(NZ - 1, lambda i: z_wait_from(a, i))

    z_start(0)
    z_start(1)

    lane = lax.broadcasted_iota(jnp.int32, (ROWS, DH), 1)
    fetch[0].wait()
    fetch[1].wait()
    numbers = doc_in[...].reshape(1, CTX_ROWS)
    counts = jnp.zeros((1, DH), F32)
    for d in range(3):
        before = jnp.sum((numbers <= d).astype(F32), axis=1, keepdims=True)
        counts = jnp.where(lane[:1] == d, before, counts)
    stats[...] = jnp.concatenate([lse_in[...], counts], axis=1)

    @pl.when(hub)
    def _():
        lse_own.start()

    @pl.when(jnp.logical_not(hub))
    def _():
        lse_copy(z).start()

    z_start(2)
    z_start(3)

    fetch[2].wait()
    fetch[3].wait()
    sums = jnp.zeros((ROWS, DH), F32)
    for h in range(NZ):
        cols = block(h, DH)
        row = jnp.sum(g_in[:, cols].astype(F32) * o_in[:, cols].astype(F32), axis=1, keepdims=True)
        sums = jnp.where(lane == h, row, sums)
    turned = jnp.concatenate([sums, jnp.zeros((DH - ROWS, DH), F32)], axis=0).T
    for h in range(NZ):
        delta[h] = turned[h : h + 1, :]

    def delta_copy(i, to, frm):
        return remote(
            delta.at[to], D.at[frm, c, y], d_send.at[i], d_recv.at[frm], device(x, y, ring(z, i, NZ), c)
        )

    delta_own = pltpu.make_async_copy(delta.at[z], D.at[z, c, y], own.at[6])
    delta_own.start()
    loop(NZ - 1, lambda i: delta_copy(i, ring(z, i, NZ), z).start())

    def sib_copy(part, slot):
        return remote(part, part, s_send.at[slot], s_recv.at[slot], sib)

    ys = (Q, G, D)

    def y_copy(a, i, frm, to):
        part = ys[a].at[:, c, frm]
        return remote(part, part, y_send.at[a, i], y_recv.at[a, frm], device(x, to, z, c))

    def sib_y(a, frm, core):
        return sib_copy(ys[a].at[:, core, frm], a * NY + frm)

    def y_start(a):
        for i in range(NY - 1):
            y_copy(a, i, y, ring(y, i, NY)).start()
        sib_y(a, y, c).start()

    def y_relay(a):
        for i in range(NY - 1):
            frm = ring(y, i, NY)
            y_copy(a, i, frm, y).wait_recv()
            sib_y(a, frm, c).start()

    def y_wait(a):
        for frm in range(NY):
            sib_y(a, frm, 1 - c).wait_recv()

    def x_copy(i, frm, to):
        part = K.at[:, frm]
        return remote(part, part, x_send.at[i], x_recv.at[frm], device(to, y, z, c))

    def xv_copy(i, zs, frm, to):
        part = V.at[zs, frm]
        return remote(part, part, xv_send.at[i, zs], xv_recv.at[frm, zs], device(to, y, z, c))

    def xv_start(zs):
        for i in range(NX - 1):
            xv_copy(i, zs, x, ring(x, i, NX)).start()

    def pass_values(first, last):
        def one(i):
            z_wait_from(3, first + i)
            xv_start(ring(z, first + i, NZ))

        loop(last - first, one)

    def plane_copy(i):
        return remote(L.at[c], L.at[c], plane_send.at[i], plane_recv, plane_peer(i))

    def lse_sib(core):
        return sib_copy(L.at[core], 3 * NY)

    @pl.when(hub)
    def _():
        lse_own.wait()

        def one(i):
            lse_copy(ring(z, i, NZ)).wait_recv()

        loop(NZ - 1, one)
        loop(NX * NY - 1, lambda i: plane_copy(i).start())

    z_wait(0)
    y_start(0)
    z_wait(1)
    for i in range(NX - 1):
        x_copy(i, x, ring(x, i, NX)).start()

    @pl.when(jnp.logical_not(hub))
    def _():
        plane_copy(0).wait_recv()

    lse_sib(c).start()
    z_wait(2)
    y_start(1)
    y_relay(0)
    delta_own.wait()
    loop(NZ - 1, lambda i: delta_copy(i, z, ring(z, i, NZ)).wait_recv())
    y_start(2)
    lse_sib(1 - c).wait_recv()
    rows = [jnp.concatenate([L[core, zz] for zz in range(NZ)], axis=0) for core in range(NC)]
    counts = rows[0][:, CTX_ROWS:] + rows[1][:, CTX_ROWS:]
    ends = [jnp.sum(counts[:, d : d + 1]).astype(jnp.int32) for d in range(3)]

    def doc_start(pos):
        start = jnp.where(pos >= ends[0], ends[0], 0)
        start = jnp.where(pos >= ends[1], ends[1], start)
        return jnp.where(pos >= ends[2], ends[2], start)

    def lay_rows(by_plane, out):
        for j in range(N_BLK):
            out[j] = jnp.concatenate([by_plane[zz : zz + 1] for zz in range(BLK * j, BLK * (j + 1))], axis=1)

    parts = []
    for core in range(NC):
        picked = rows[core][:, :PART]
        for xx in range(1, NX):
            picked = jnp.where(x == xx, rows[core][:, block(xx, PART)], picked)
        parts.append(picked)
    lay_rows(jnp.concatenate(parts, axis=1), lse_s)

    q_at = lax.broadcasted_iota(jnp.int32, (1, Q_BLK), 1)
    q_in = lax.rem(q_at, Q_Z)
    q_base = (
        lax.div(q_at, Q_Z) * SPAN + lax.div(q_in, PART) * CTX_ROWS + x * PART + lax.rem(q_in, PART)
    )
    k_at = lax.broadcasted_iota(jnp.int32, (K_BLK, 1), 0)
    k_in = lax.rem(k_at, K_Z)
    k_base = (
        lax.div(k_at, K_Z) * SPAN
        + c * CTX_ROWS
        + lax.div(k_in, ROWS) * PART
        + y * ROWS
        + lax.rem(k_in, ROWS)
    )

    def flat(src, out, rows):
        def step(zz):
            at = pl.ds(pl.multiple_of(zz * rows, rows), rows)
            out[at, :] = src[zz].astype(F32).reshape(rows, DH).astype(BF16)

        loop(NZ, step)

    y_wait(0)
    flat(Q, qs, Q_Z)
    for i in range(NX - 1):
        x_copy(i, ring(x, i, NX), x).wait_recv()
    flat(K, ks, K_Z)

    def probs_block(j):
        q_pos = q_base + j * (BLK * SPAN)
        start = doc_start(q_pos)
        for i in range(j + 1):
            k_pos = k_base + i * (BLK * SPAN)
            allowed = jnp.where(k_pos < ends[0], NZ * SPAN, k_pos) >= start
            if i == j:
                allowed = allowed & (k_pos <= q_pos)
            s = contract_last(ks[block(i, K_BLK), :], qs[block(j, Q_BLK), :])
            p = jnp.where(allowed, jnp.exp(s * scale - lse_s[j]), 0.0)
            probs[block(i, K_BLK), block(j, Q_BLK)] = p.astype(BF16)

    probs_block(0)
    probs_block(1)
    own_copy(3).wait()
    xv_start(z)
    pass_values(0, 8)
    probs_block(2)
    pass_values(8, NZ - 1)
    y_relay(1)
    probs_block(3)
    y_relay(2)

    y_wait(1)
    flat(G, gs, Q_Z)

    def v_copy(i, frm, to):
        return remote(dv.at[:, to], rv.at[frm], v_send.at[i], v_recv.at[frm], device(to, y, z, c))

    for i in range(N_BLK):
        total = jnp.dot(
            probs[block(i, K_BLK), i * Q_BLK :], gs[i * Q_BLK :, :], preferred_element_type=F32
        )
        dv[BLK * i : BLK * (i + 1)] = total.reshape(BLK, NX, ROWS, DH).astype(BF16)
    for i in range(NX - 1):
        v_copy(i, x, ring(x, i, NX)).start()

    y_wait(2)
    parts = []
    for core in range(NC):
        for yy in range(NY):
            parts.append(jnp.concatenate([D[zz, core, yy] for zz in range(NZ)], axis=0)[:, :ROWS])
    lay_rows(jnp.concatenate(parts, axis=1), delta_s)
    for i in range(N_BLK):
        kt[i] = ks[block(i, K_BLK), :].T
    for i in range(NX - 1):
        loop(NZ, lambda zs, i=i: xv_copy(i, zs, ring(x, i, NX), x).wait_recv())
    flat(V, vs, K_Z)

    def k_copy(j, i, frm, to):
        rows = pl.ds(BLK * j, BLK)
        return remote(
            dk.at[rows, to], rk.at[frm, rows], k_send.at[j, i], k_recv.at[j, frm], device(to, y, z, c)
        )

    def p_copy(j, core):
        rows = pl.ds(BLK * j, BLK)
        return remote(dq.at[rows, core], rs.at[rows], p_send.at[j], p_recv.at[j], sib)

    def q_copy(j, i, frm, to):
        rows = pl.ds(BLK * j, BLK)
        return remote(
            pq.at[rows, to], rq.at[frm, rows], q_send.at[j, i], q_recv.at[j, frm], device(x, to, z, c)
        )

    def grads_block(j):
        total = jnp.zeros((DH, Q_BLK), F32)
        for i in range(j + 1):
            dp = contract_last(vs[block(i, K_BLK), :], gs[block(j, Q_BLK), :])
            p = probs[block(i, K_BLK), block(j, Q_BLK)].astype(F32)
            ds = (p * (dp - delta_s[j])).astype(BF16)
            probs[block(i, K_BLK), block(j, Q_BLK)] = ds
            total += jnp.dot(kt[i], ds, preferred_element_type=F32)
        dq[BLK * j : BLK * (j + 1)] = total.T.reshape(BLK, NC, NY, ROWS, DH).astype(BF16)
        p_copy(j, 1 - c).start()
        total = jnp.dot(
            probs[block(j, K_BLK), j * Q_BLK :], qs[j * Q_BLK :, :], preferred_element_type=F32
        )
        dk[BLK * j : BLK * (j + 1)] = total.reshape(BLK, NX, ROWS, DH).astype(BF16)
        for i in range(NX - 1):
            k_copy(j, i, x, ring(x, i, NX)).start()

    outs = (oq, ok, ov)

    def home_copy(a, to, frm):
        return remote(
            res.at[a, to], outs[a].at[:, columns(frm)], h_send.at[a, to], h_recv.at[a, frm],
            device(x, y, to, c),
        )

    def home_own(a):
        return pltpu.make_async_copy(res.at[a, z], outs[a].at[:, columns(z)], own.at[7 + a])

    def send_home(a, to):
        @pl.when(to == z)
        def _():
            home_own(a).start()

        @pl.when(to != z)
        def _():
            home_copy(a, to, z).start()

    def add_v():
        for i in range(NX - 1):
            v_copy(i, ring(x, i, NX), x).wait_recv()

        def one(zz):
            total = dv[zz, x].astype(F32)
            for i in range(NX - 1):
                total += rv[ring(x, i, NX), zz].astype(F32)
            res[2, zz] = total.astype(BF16)

        loop(NZ, one)
        loop(NZ, lambda i: send_home(2, lax.rem(z + i, NZ)))

    def pair_block(j):
        p_copy(j, c).wait_recv()

        def one(step):
            zz = BLK * j + step
            pq[zz] = (dq[zz, c].astype(F32) + rs[zz].astype(F32)).astype(BF16)

        loop(BLK, one)
        for i in range(NY - 1):
            q_copy(j, i, y, ring(y, i, NY)).start()

    def add_block(j):
        for i in range(NX - 1):
            k_copy(j, i, ring(x, i, NX), x).wait_recv()
        for i in range(NY - 1):
            q_copy(j, i, ring(y, i, NY), y).wait_recv()

        def one(step):
            zz = BLK * j + step
            total = dk[zz, x].astype(F32)
            for i in range(NX - 1):
                total += rk[ring(x, i, NX), zz].astype(F32)
            res[1, zz] = (total * scale).astype(BF16)
            total = pq[zz, y].astype(F32)
            for i in range(NY - 1):
                total += rq[ring(y, i, NY), zz].astype(F32)
            res[0, zz] = (total * scale).astype(BF16)
            send_home(1, zz)
            send_home(0, zz)

        loop(BLK, one)

    grads_block(3)
    grads_block(2)
    pair_block(3)
    grads_block(1)
    pair_block(2)
    add_v()
    grads_block(0)
    pair_block(1)
    pair_block(0)
    add_block(3)
    add_block(2)
    add_block(1)
    add_block(0)

    for a in range(4):
        loop(NZ - 1, lambda i, a=a: z_copy(a, i).wait_send())
    loop(NZ - 1, lambda i: delta_copy(i, ring(z, i, NZ), z).wait_send())

    @pl.when(jnp.logical_not(hub))
    def _():
        lse_copy(z).wait_send()

    @pl.when(hub)
    def _():
        loop(NX * NY - 1, lambda i: plane_copy(i).wait_send())

    for i in range(NX - 1):
        x_copy(i, x, ring(x, i, NX)).wait_send()
        loop(NZ, lambda zs, i=i: xv_copy(i, zs, x, ring(x, i, NX)).wait_send())
    for a in range(3):
        for i in range(NY - 1):
            y_copy(a, i, y, ring(y, i, NY)).wait_send()
        for frm in range(NY):
            sib_y(a, frm, c).wait_send()
    lse_sib(c).wait_send()
    for i in range(NX - 1):
        v_copy(i, x, ring(x, i, NX)).wait_send()
    for j in range(N_BLK):
        for i in range(NX - 1):
            k_copy(j, i, x, ring(x, i, NX)).wait_send()
        for i in range(NY - 1):
            q_copy(j, i, y, ring(y, i, NY)).wait_send()
        p_copy(j, 1 - c).wait_send()
    for a in range(3):
        home_own(a).wait()

        def one(i, a=a):
            peer = ring(z, i, NZ)
            home_copy(a, peer, z).wait_send()
            home_copy(a, z, peer).wait_recv()

        loop(NZ - 1, one)


def copy_kernel(a, b, c, out_a, out_b, out_c):
    out_a[...], out_b[...], out_c[...] = a[...], b[...], c[...]


def copied(grads):
    vmem = pl.BlockSpec(memory_space=pltpu.VMEM)
    out = jax.ShapeDtypeStruct((ROWS, NZ * DH), BF16)
    return pl.pallas_call(
        copy_kernel, out_shape=(out,) * 3, in_specs=[vmem] * 3, out_specs=(vmem,) * 3, name="copy_grads"
    )(*grads)


def per_device(queries, keys, values, outputs, grad_out, log_sums, doc_ids):
    dma = pltpu.SemaphoreType.DMA
    hbm = pl.BlockSpec(memory_space=pl.ANY)
    out = jax.ShapeDtypeStruct((ROWS, NZ * DH), BF16)
    kv, qg = (NZ, NX, ROWS, DH), (NZ, NC, NY, ROWS, DH)
    grads = pl.pallas_call(
        kernel,
        out_shape=(out, out, out),
        in_specs=[pl.BlockSpec(memory_space=pltpu.HBM)] * 7,
        out_specs=(hbm,) * 3,
        scratch_shapes=[
            pltpu.VMEM(qg, BF16), pltpu.VMEM(kv, BF16), pltpu.VMEM(kv, BF16), pltpu.VMEM(qg, BF16),
            pltpu.VMEM((NC, NZ, 1, STATS), F32),
            pltpu.VMEM((NZ, NC, NY, 1, DH), F32),
            pltpu.VMEM((NZ, 1, DH), F32), pltpu.VMEM((1, STATS), F32),
            pltpu.VMEM((CTX_ROWS,), jnp.int32), pltpu.VMEM((1, CTX_ROWS), F32), pltpu.VMEM((ROWS, NZ * DH), BF16), pltpu.VMEM((ROWS, NZ * DH), BF16),
            pltpu.VMEM((NZ * Q_Z, DH), BF16), pltpu.VMEM((NZ * K_Z, DH), BF16),
            pltpu.VMEM((NZ * K_Z, DH), BF16), pltpu.VMEM((NZ * Q_Z, DH), BF16),
            pltpu.VMEM((N_BLK, DH, K_BLK), BF16), pltpu.VMEM((NZ * K_Z, NZ * Q_Z), BF16),
            pltpu.VMEM((N_BLK, 1, Q_BLK), F32), pltpu.VMEM((N_BLK, 1, Q_BLK), F32),
            pltpu.VMEM(qg, BF16), pltpu.VMEM(kv, BF16), pltpu.VMEM(kv, BF16),
            pltpu.VMEM((NZ, NY, ROWS, DH), BF16), pltpu.VMEM((NZ, NY, ROWS, DH), BF16),
            pltpu.VMEM((NY, NZ, ROWS, DH), BF16),
            pltpu.VMEM((NX, NZ, ROWS, DH), BF16), pltpu.VMEM((NX, NZ, ROWS, DH), BF16),
            pltpu.VMEM((3, NZ, ROWS, DH), BF16),
            dma((4, NZ - 1)), dma((4, NZ)), dma((14,)),
            dma((NZ - 1,)), dma((NZ,)),
            dma, dma((NZ,)), dma((NX * NY - 1,)), dma,
            dma((NX - 1,)), dma((NX,)), dma((3, NY - 1)), dma((3, NY)),
            dma((3 * NY + 1,)), dma((3 * NY + 1,)),
            dma((NX - 1, NZ)), dma((NX, NZ)), dma((N_BLK,)), dma((N_BLK,)),
            dma((N_BLK, NY - 1)), dma((N_BLK, NY)), dma((N_BLK, NX - 1)), dma((N_BLK, NX)),
            dma((NX - 1,)), dma((NX,)), dma((3, NZ)), dma((3, NZ)),
        ],
        compiler_params=pltpu.CompilerParams(
            collective_id=0, has_side_effects=True, vmem_limit_bytes=60 * 1024 * 1024
        ),
        name="attention_grads",
    )(queries, keys, values, outputs, grad_out, log_sums, doc_ids)
    return copied(grads)


def solution(mesh):
    tokens = P(("ctx", "head"), None)
    return jax.shard_map(
        per_device,
        mesh=mesh,
        in_specs=(tokens,) * 5 + (P("head", "ctx"), P("ctx")),
        out_specs=(tokens,) * 3,
        check_vma=False,
    )
```

```python
import jax
import jax.numpy as jnp
from jax import lax
from jax.experimental import pallas as pl
from jax.experimental.pallas import tpu as pltpu
from jax.sharding import PartitionSpec as P

DH = 128
NX, NY, NZ, NC = 4, 4, 16, 2
ROWS = 24
CTX_ROWS = NX * NY * ROWS
SPAN = NC * CTX_ROWS
Q_Z = NC * NY * ROWS
K_Z = NX * ROWS
BLK = 4
N_BLK = NZ // BLK
Q_BLK = BLK * Q_Z
K_BLK = BLK * K_Z
PART = NY * ROWS
MESH = pl.DeviceIdType.MESH
F32 = jnp.float32
BF16 = jnp.bfloat16


def here():
    ctx, head = lax.axis_index("ctx"), lax.axis_index("head")
    return lax.div(head, NY), lax.rem(head, NY), lax.div(ctx, NC), lax.rem(ctx, NC)


def device(x, y, z, c):
    return (z * NC + c, x * NY + y)


def ring(me, step, size):
    away = lax.div(step, 2) + 1
    return lax.rem(jnp.where(lax.rem(step, 2) == 0, me + away, me - away + size), size)


def columns(head):
    return pl.ds(pl.multiple_of(head * DH, DH), DH)


def remote(src, dst, send, recv, to):
    return pltpu.make_async_remote_copy(
        src_ref=src, dst_ref=dst, send_sem=send, recv_sem=recv, device_id=to, device_id_type=MESH
    )


def loop(count, body):
    def step(i, carry):
        body(i)
        return carry

    lax.fori_loop(0, count, step, 0)


def contract_last(left, right):
    return lax.dot_general(left, right, (((1,), (1,)), ((), ())), preferred_element_type=F32)


def block(i, size):
    return slice(i * size, (i + 1) * size)


def kernel(
    q, k, v, o, g, lse, doc,
    oq, ok, ov,
    Q, K, V, G, LH, L, D, delta, stats, doc_in, lse_in, g_in, o_in,
    qs, ks, vs, gs, kt, probs, lse_s, delta_s,
    dq, dk, dv, pq, rs, rq, rk, rv, res,
    z_send, z_recv, own, d_send, d_recv,
    hub_send, hub_recv, plane_send, plane_recv,
    x_send, x_recv, y_send, y_recv, s_send, s_recv,
    xv_send, xv_recv, p_send, p_recv,
    q_send, q_recv, k_send, k_recv, v_send, v_recv, h_send, h_recv,
):
    x, y, z, c = here()
    plane = x * NY + y
    sib = device(x, y, z, 1 - c)
    hub = z == plane
    scale = DH**-0.5

    barrier = pltpu.get_barrier_semaphore()

    def greet(to):
        pl.semaphore_signal(barrier, inc=1, device_id=to, device_id_type=MESH)

    def plane_peer(i):
        other = lax.rem(plane + i + 1, NX * NY)
        return device(lax.div(other, NY), lax.rem(other, NY), z, c)

    loop(NZ - 1, lambda i: greet(device(x, y, ring(z, i, NZ), c)))
    fetch = [
        pltpu.make_async_copy(src, dst, own.at[10 + i])
        for i, (src, dst) in enumerate(((doc, doc_in), (lse, lse_in), (g, g_in), (o, o_in)))
    ]
    for copy in fetch:
        copy.start()
    loop(NX - 1, lambda i: greet(device(ring(x, i, NX), y, z, c)))
    loop(NY - 1, lambda i: greet(device(x, ring(y, i, NY), z, c)))
    greet(sib)

    @pl.when(hub)
    def _():
        loop(NX * NY - 1, lambda i: greet(plane_peer(i)))

    @pl.when(jnp.logical_not(hub))
    def _():
        greet(device(lax.div(z, NY), lax.rem(z, NY), z, c))

    pl.semaphore_wait(
        barrier, NZ - 1 + NX - 1 + NY - 1 + 1 + jnp.where(hub, NX * NY - 1, 1)
    )

    def lse_copy(frm):
        return remote(stats, LH.at[frm], hub_send, hub_recv.at[frm], device(x, y, plane, c))

    lse_own = pltpu.make_async_copy(stats, LH.at[z], own.at[4])

    srcs = (q, k, g, v)

    def landing(a, zs):
        return (Q.at[zs, c, y], K.at[zs, x], G.at[zs, c, y], V.at[zs, x])[a]

    def z_copy(a, i):
        to = ring(z, i, NZ)
        return remote(
            srcs[a].at[:, columns(to)], landing(a, z), z_send.at[a, i], z_recv.at[a, z],
            device(x, y, to, c),
        )

    def own_copy(a):
        return pltpu.make_async_copy(srcs[a].at[:, columns(z)], landing(a, z), own.at[a])

    def z_start(a):
        own_copy(a).start()
        loop(NZ - 1, lambda i: z_copy(a, i).start())

    def z_wait_from(a, i):
        frm = ring(z, i, NZ)
        remote(
            srcs[a].at[:, columns(frm)], landing(a, frm), z_send.at[a, i], z_recv.at[a, frm],
            device(x, y, frm, c),
        ).wait_recv()

    def z_wait(a):
        own_copy(a).wait()
        loop(NZ - 1, lambda i: z_wait_from(a, i))

    z_start(0)

    lane = lax.broadcasted_iota(jnp.int32, (ROWS, DH), 1)
    fetch[0].wait()
    fetch[1].wait()
    numbers = doc_in[...].reshape(1, CTX_ROWS)
    counts = jnp.zeros((1, DH), F32)
    for d in range(3):
        before = jnp.sum((numbers <= d).astype(F32), axis=1, keepdims=True)
        counts = jnp.where(lane[:1] == d, before, counts)
    for xx in range(NX):
        stats[xx] = jnp.concatenate([lse_in[:, block(xx, PART)], counts[:, : DH - PART]], axis=1)

    @pl.when(hub)
    def _():
        lse_own.start()

    @pl.when(jnp.logical_not(hub))
    def _():
        lse_copy(z).start()

    z_start(1)

    fetch[2].wait()
    fetch[3].wait()
    sums = jnp.zeros((ROWS, DH), F32)
    for h in range(NZ):
        cols = block(h, DH)
        row = jnp.sum(g_in[:, cols].astype(F32) * o_in[:, cols].astype(F32), axis=1, keepdims=True)
        sums = jnp.where(lane == h, row, sums)
    turned = jnp.concatenate([sums, jnp.zeros((DH - ROWS, DH), F32)], axis=0).T
    for h in range(NZ):
        delta[h] = turned[h : h + 1, :]

    def delta_copy(i, to, frm):
        return remote(
            delta.at[to], D.at[frm, c, y], d_send.at[i], d_recv.at[frm], device(x, y, ring(z, i, NZ), c)
        )

    delta_own = pltpu.make_async_copy(delta.at[z], D.at[z, c, y], own.at[6])
    delta_own.start()
    loop(NZ - 1, lambda i: delta_copy(i, ring(z, i, NZ), z).start())
    z_start(2)
    z_start(3)

    def sib_copy(part, slot):
        return remote(part, part, s_send.at[slot], s_recv.at[slot], sib)

    ys = (Q, G, D)

    def y_copy(a, i, frm, to):
        part = ys[a].at[:, c, frm]
        return remote(part, part, y_send.at[a, i], y_recv.at[a, frm], device(x, to, z, c))

    def sib_y(a, frm, core):
        return sib_copy(ys[a].at[:, core, frm], a * NY + frm)

    def y_start(a):
        for i in range(NY - 1):
            y_copy(a, i, y, ring(y, i, NY)).start()
        sib_y(a, y, c).start()

    def y_relay(a):
        for i in range(NY - 1):
            frm = ring(y, i, NY)
            y_copy(a, i, frm, y).wait_recv()
            sib_y(a, frm, c).start()

    def y_wait(a):
        for frm in range(NY):
            sib_y(a, frm, 1 - c).wait_recv()

    def x_copy(i, frm, to):
        part = K.at[:, frm]
        return remote(part, part, x_send.at[i], x_recv.at[frm], device(to, y, z, c))

    def xv_copy(i, zs, frm, to):
        part = V.at[zs, frm]
        return remote(part, part, xv_send.at[i, zs], xv_recv.at[frm, zs], device(to, y, z, c))

    def xv_start(zs):
        for i in range(NX - 1):
            xv_copy(i, zs, x, ring(x, i, NX)).start()

    def pass_values(first, last):
        def one(i):
            z_wait_from(3, first + i)
            xv_start(ring(z, first + i, NZ))

        loop(last - first, one)

    def plane_copy(i):
        other = lax.rem(plane + i + 1, NX * NY)
        return remote(
            LH.at[:, lax.div(other, NY)], L.at[c], plane_send.at[i], plane_recv, plane_peer(i)
        )

    def lse_sib(core):
        return sib_copy(L.at[core], 3 * NY)

    z_wait(0)
    y_start(0)

    @pl.when(hub)
    def _():
        lse_own.wait()

        def one(i):
            lse_copy(ring(z, i, NZ)).wait_recv()

        loop(NZ - 1, one)
        loop(NX * NY - 1, lambda i: plane_copy(i).start())
        pltpu.make_async_copy(LH.at[:, x], L.at[c], own.at[5]).start()

    z_wait(1)
    for i in range(NX - 1):
        x_copy(i, x, ring(x, i, NX)).start()

    @pl.when(hub)
    def _():
        pltpu.make_async_copy(LH.at[:, x], L.at[c], own.at[5]).wait()

    @pl.when(jnp.logical_not(hub))
    def _():
        plane_copy(0).wait_recv()

    lse_sib(c).start()
    delta_own.wait()
    loop(NZ - 1, lambda i: delta_copy(i, z, ring(z, i, NZ)).wait_recv())
    y_start(2)
    y_relay(0)
    z_wait(2)
    y_start(1)
    lse_sib(1 - c).wait_recv()
    rows = [jnp.concatenate([L[core, zz] for zz in range(NZ)], axis=0) for core in range(NC)]
    counts = rows[0][:, PART:] + rows[1][:, PART:]
    ends = [jnp.sum(counts[:, d : d + 1]).astype(jnp.int32) for d in range(3)]

    def doc_start(pos):
        start = jnp.where(pos >= ends[0], ends[0], 0)
        start = jnp.where(pos >= ends[1], ends[1], start)
        return jnp.where(pos >= ends[2], ends[2], start)

    def lay_rows(by_plane, out):
        for j in range(N_BLK):
            out[j] = jnp.concatenate([by_plane[zz : zz + 1] for zz in range(BLK * j, BLK * (j + 1))], axis=1)

    lay_rows(jnp.concatenate([of_core[:, :PART] for of_core in rows], axis=1), lse_s)

    q_at = lax.broadcasted_iota(jnp.int32, (1, Q_BLK), 1)
    q_in = lax.rem(q_at, Q_Z)
    q_base = (
        lax.div(q_at, Q_Z) * SPAN + lax.div(q_in, PART) * CTX_ROWS + x * PART + lax.rem(q_in, PART)
    )
    k_at = lax.broadcasted_iota(jnp.int32, (K_BLK, 1), 0)
    k_in = lax.rem(k_at, K_Z)
    k_base = (
        lax.div(k_at, K_Z) * SPAN
        + c * CTX_ROWS
        + lax.div(k_in, ROWS) * PART
        + y * ROWS
        + lax.rem(k_in, ROWS)
    )

    def flat(src, out, rows):
        def step(zz):
            at = pl.ds(pl.multiple_of(zz * rows, rows), rows)
            out[at, :] = src[zz].astype(F32).reshape(rows, DH).astype(BF16)

        loop(NZ, step)

    y_wait(0)
    flat(Q, qs, Q_Z)
    for i in range(NX - 1):
        x_copy(i, ring(x, i, NX), x).wait_recv()
    flat(K, ks, K_Z)

    def probs_block(j):
        q_pos = q_base + j * (BLK * SPAN)
        start = doc_start(q_pos)
        for i in range(j + 1):
            k_pos = k_base + i * (BLK * SPAN)
            allowed = jnp.where(k_pos < ends[0], NZ * SPAN, k_pos) >= start
            if i == j:
                allowed = allowed & (k_pos <= q_pos)
            s = contract_last(ks[block(i, K_BLK), :], qs[block(j, Q_BLK), :])
            p = jnp.where(allowed, jnp.exp(s * scale - lse_s[j]), 0.0)
            probs[block(i, K_BLK), block(j, Q_BLK)] = p.astype(BF16)

    probs_block(0)
    probs_block(1)
    own_copy(3).wait()
    xv_start(z)
    pass_values(0, 8)
    probs_block(2)
    pass_values(8, NZ - 1)
    y_relay(1)
    probs_block(3)
    y_relay(2)

    y_wait(1)
    flat(G, gs, Q_Z)

    def v_copy(i, frm, to):
        return remote(dv.at[:, to], rv.at[frm], v_send.at[i], v_recv.at[frm], device(to, y, z, c))

    for i in range(N_BLK):
        total = jnp.dot(
            probs[block(i, K_BLK), i * Q_BLK :], gs[i * Q_BLK :, :], preferred_element_type=F32
        )
        dv[BLK * i : BLK * (i + 1)] = total.reshape(BLK, NX, ROWS, DH).astype(BF16)
    for i in range(NX - 1):
        v_copy(i, x, ring(x, i, NX)).start()

    y_wait(2)
    parts = []
    for core in range(NC):
        for yy in range(NY):
            parts.append(jnp.concatenate([D[zz, core, yy] for zz in range(NZ)], axis=0)[:, :ROWS])
    lay_rows(jnp.concatenate(parts, axis=1), delta_s)
    for i in range(N_BLK):
        kt[i] = ks[block(i, K_BLK), :].T
    for i in range(NX - 1):
        loop(NZ, lambda zs, i=i: xv_copy(i, zs, ring(x, i, NX), x).wait_recv())
    flat(V, vs, K_Z)

    def k_copy(j, i, frm, to):
        rows = pl.ds(BLK * j, BLK)
        return remote(
            dk.at[rows, to], rk.at[frm, rows], k_send.at[j, i], k_recv.at[j, frm], device(to, y, z, c)
        )

    def p_copy(j, core):
        rows = pl.ds(BLK * j, BLK)
        return remote(dq.at[rows, core], rs.at[rows], p_send.at[j], p_recv.at[j], sib)

    def q_copy(j, i, frm, to):
        rows = pl.ds(BLK * j, BLK)
        return remote(
            pq.at[rows, to], rq.at[frm, rows], q_send.at[j, i], q_recv.at[j, frm], device(x, to, z, c)
        )

    def grads_block(j):
        total = jnp.zeros((DH, Q_BLK), F32)
        for i in range(j + 1):
            dp = contract_last(vs[block(i, K_BLK), :], gs[block(j, Q_BLK), :])
            p = probs[block(i, K_BLK), block(j, Q_BLK)].astype(F32)
            ds = (p * (dp - delta_s[j])).astype(BF16)
            probs[block(i, K_BLK), block(j, Q_BLK)] = ds
            total += jnp.dot(kt[i], ds, preferred_element_type=F32)
        dq[BLK * j : BLK * (j + 1)] = total.T.reshape(BLK, NC, NY, ROWS, DH).astype(BF16)
        p_copy(j, 1 - c).start()
        total = jnp.dot(
            probs[block(j, K_BLK), j * Q_BLK :], qs[j * Q_BLK :, :], preferred_element_type=F32
        )
        dk[BLK * j : BLK * (j + 1)] = total.reshape(BLK, NX, ROWS, DH).astype(BF16)
        for i in range(NX - 1):
            k_copy(j, i, x, ring(x, i, NX)).start()

    outs = (oq, ok, ov)

    def home_copy(a, to, frm):
        return remote(
            res.at[a, to], outs[a].at[:, columns(frm)], h_send.at[a, to], h_recv.at[a, frm],
            device(x, y, to, c),
        )

    def home_own(a):
        return pltpu.make_async_copy(res.at[a, z], outs[a].at[:, columns(z)], own.at[7 + a])

    def send_home(a, to):
        @pl.when(to == z)
        def _():
            home_own(a).start()

        @pl.when(to != z)
        def _():
            home_copy(a, to, z).start()

    def add_v():
        for i in range(NX - 1):
            v_copy(i, ring(x, i, NX), x).wait_recv()

        def one(zz):
            total = dv[zz, x].astype(F32)
            for i in range(NX - 1):
                total += rv[ring(x, i, NX), zz].astype(F32)
            res[2, zz] = total.astype(BF16)

        loop(NZ, one)
        loop(NZ, lambda i: send_home(2, lax.rem(z + i, NZ)))

    def pair_block(j):
        p_copy(j, c).wait_recv()

        def one(step):
            zz = BLK * j + step
            pq[zz] = (dq[zz, c].astype(F32) + rs[zz].astype(F32)).astype(BF16)

        loop(BLK, one)
        for i in range(NY - 1):
            q_copy(j, i, y, ring(y, i, NY)).start()

    def add_block(j):
        for i in range(NX - 1):
            k_copy(j, i, ring(x, i, NX), x).wait_recv()
        for i in range(NY - 1):
            q_copy(j, i, ring(y, i, NY), y).wait_recv()

        def one(step):
            zz = BLK * j + step
            total = dk[zz, x].astype(F32)
            for i in range(NX - 1):
                total += rk[ring(x, i, NX), zz].astype(F32)
            res[1, zz] = (total * scale).astype(BF16)
            total = pq[zz, y].astype(F32)
            for i in range(NY - 1):
                total += rq[ring(y, i, NY), zz].astype(F32)
            res[0, zz] = (total * scale).astype(BF16)
            send_home(1, zz)
            send_home(0, zz)

        loop(BLK, one)

    grads_block(3)
    grads_block(2)
    pair_block(3)
    grads_block(1)
    pair_block(2)
    add_v()
    grads_block(0)
    pair_block(1)
    pair_block(0)
    add_block(3)
    add_block(2)
    add_block(1)
    add_block(0)

    for a in range(4):
        loop(NZ - 1, lambda i, a=a: z_copy(a, i).wait_send())
    loop(NZ - 1, lambda i: delta_copy(i, ring(z, i, NZ), z).wait_send())

    @pl.when(jnp.logical_not(hub))
    def _():
        lse_copy(z).wait_send()

    @pl.when(hub)
    def _():
        loop(NX * NY - 1, lambda i: plane_copy(i).wait_send())

    for i in range(NX - 1):
        x_copy(i, x, ring(x, i, NX)).wait_send()
        loop(NZ, lambda zs, i=i: xv_copy(i, zs, x, ring(x, i, NX)).wait_send())
    for a in range(3):
        for i in range(NY - 1):
            y_copy(a, i, y, ring(y, i, NY)).wait_send()
        for frm in range(NY):
            sib_y(a, frm, c).wait_send()
    lse_sib(c).wait_send()
    for i in range(NX - 1):
        v_copy(i, x, ring(x, i, NX)).wait_send()
    for j in range(N_BLK):
        for i in range(NX - 1):
            k_copy(j, i, x, ring(x, i, NX)).wait_send()
        for i in range(NY - 1):
            q_copy(j, i, y, ring(y, i, NY)).wait_send()
        p_copy(j, 1 - c).wait_send()
    for a in range(3):
        home_own(a).wait()

        def one(i, a=a):
            peer = ring(z, i, NZ)
            home_copy(a, peer, z).wait_send()
            home_copy(a, z, peer).wait_recv()

        loop(NZ - 1, one)


def copy_kernel(a, b, c, out_a, out_b, out_c):
    out_a[...], out_b[...], out_c[...] = a[...], b[...], c[...]


def copied(grads):
    vmem = pl.BlockSpec(memory_space=pltpu.VMEM)
    out = jax.ShapeDtypeStruct((ROWS, NZ * DH), BF16)
    return pl.pallas_call(
        copy_kernel, out_shape=(out,) * 3, in_specs=[vmem] * 3, out_specs=(vmem,) * 3, name="copy_grads"
    )(*grads)


def per_device(queries, keys, values, outputs, grad_out, log_sums, doc_ids):
    dma = pltpu.SemaphoreType.DMA
    hbm = pl.BlockSpec(memory_space=pl.ANY)
    out = jax.ShapeDtypeStruct((ROWS, NZ * DH), BF16)
    kv, qg = (NZ, NX, ROWS, DH), (NZ, NC, NY, ROWS, DH)
    grads = pl.pallas_call(
        kernel,
        out_shape=(out, out, out),
        in_specs=[pl.BlockSpec(memory_space=pltpu.HBM)] * 7,
        out_specs=(hbm,) * 3,
        scratch_shapes=[
            pltpu.VMEM(qg, BF16), pltpu.VMEM(kv, BF16), pltpu.VMEM(kv, BF16), pltpu.VMEM(qg, BF16),
            pltpu.VMEM((NZ, NX, 1, DH), F32), pltpu.VMEM((NC, NZ, 1, DH), F32),
            pltpu.VMEM((NZ, NC, NY, 1, DH), F32),
            pltpu.VMEM((NZ, 1, DH), F32), pltpu.VMEM((NX, 1, DH), F32),
            pltpu.VMEM((CTX_ROWS,), jnp.int32), pltpu.VMEM((1, CTX_ROWS), F32), pltpu.VMEM((ROWS, NZ * DH), BF16), pltpu.VMEM((ROWS, NZ * DH), BF16),
            pltpu.VMEM((NZ * Q_Z, DH), BF16), pltpu.VMEM((NZ * K_Z, DH), BF16),
            pltpu.VMEM((NZ * K_Z, DH), BF16), pltpu.VMEM((NZ * Q_Z, DH), BF16),
            pltpu.VMEM((N_BLK, DH, K_BLK), BF16), pltpu.VMEM((NZ * K_Z, NZ * Q_Z), BF16),
            pltpu.VMEM((N_BLK, 1, Q_BLK), F32), pltpu.VMEM((N_BLK, 1, Q_BLK), F32),
            pltpu.VMEM(qg, BF16), pltpu.VMEM(kv, BF16), pltpu.VMEM(kv, BF16),
            pltpu.VMEM((NZ, NY, ROWS, DH), BF16), pltpu.VMEM((NZ, NY, ROWS, DH), BF16),
            pltpu.VMEM((NY, NZ, ROWS, DH), BF16),
            pltpu.VMEM((NX, NZ, ROWS, DH), BF16), pltpu.VMEM((NX, NZ, ROWS, DH), BF16),
            pltpu.VMEM((3, NZ, ROWS, DH), BF16),
            dma((4, NZ - 1)), dma((4, NZ)), dma((14,)),
            dma((NZ - 1,)), dma((NZ,)),
            dma, dma((NZ,)), dma((NX * NY - 1,)), dma,
            dma((NX - 1,)), dma((NX,)), dma((3, NY - 1)), dma((3, NY)),
            dma((3 * NY + 1,)), dma((3 * NY + 1,)),
            dma((NX - 1, NZ)), dma((NX, NZ)), dma((N_BLK,)), dma((N_BLK,)),
            dma((N_BLK, NY - 1)), dma((N_BLK, NY)), dma((N_BLK, NX - 1)), dma((N_BLK, NX)),
            dma((NX - 1,)), dma((NX,)), dma((3, NZ)), dma((3, NZ)),
        ],
        compiler_params=pltpu.CompilerParams(
            collective_id=0, has_side_effects=True, vmem_limit_bytes=60 * 1024 * 1024
        ),
        name="attention_grads",
    )(queries, keys, values, outputs, grad_out, log_sums, doc_ids)
    return copied(grads)


def solution(mesh):
    tokens = P(("ctx", "head"), None)
    return jax.shard_map(
        per_device,
        mesh=mesh,
        in_specs=(tokens,) * 5 + (P("head", "ctx"), P("ctx")),
        out_specs=(tokens,) * 3,
        check_vma=False,
    )
```

```python
import jax
import jax.numpy as jnp
from jax import lax
from jax.experimental import pallas as pl
from jax.experimental.pallas import tpu as pltpu
from jax.sharding import PartitionSpec as P

DH = 128
NX, NY, NZ, NC = 4, 4, 16, 2
ROWS = 24
CTX_ROWS = NX * NY * ROWS
SPAN = NC * CTX_ROWS
Q_Z = NC * NY * ROWS
K_Z = NX * ROWS
BLK = 4
N_BLK = NZ // BLK
Q_BLK = BLK * Q_Z
K_BLK = BLK * K_Z
PART = NY * ROWS
MESH = pl.DeviceIdType.MESH
F32 = jnp.float32
BF16 = jnp.bfloat16


def here():
    ctx, head = lax.axis_index("ctx"), lax.axis_index("head")
    return lax.div(head, NY), lax.rem(head, NY), lax.div(ctx, NC), lax.rem(ctx, NC)


def device(x, y, z, c):
    return (z * NC + c, x * NY + y)


def ring(me, step, size):
    away, up = step if isinstance(step, tuple) else (step // 2 + 1, step % 2 == 0)
    if up:
        return jnp.where(me + away >= size, me + away - size, me + away)
    return jnp.where(me < away, me - away + size, me - away)


def slot(step):
    away, up = step
    return 2 * (away - 1) + (0 if up else 1)


def peers(body):
    def step(i, carry):
        body((i + 1, True))
        body((i + 1, False))
        return carry

    lax.fori_loop(0, NZ // 2 - 1, step, 0)
    body((NZ // 2, True))


def columns(head):
    return pl.ds(pl.multiple_of(head * DH, DH), DH)


def remote(src, dst, send, recv, to):
    return pltpu.make_async_remote_copy(
        src_ref=src, dst_ref=dst, send_sem=send, recv_sem=recv, device_id=to, device_id_type=MESH
    )


def loop(count, body):
    def step(i, carry):
        body(i)
        return carry

    lax.fori_loop(0, count, step, 0)


def contract_last(left, right):
    return lax.dot_general(left, right, (((1,), (1,)), ((), ())), preferred_element_type=F32)


def block(i, size):
    return slice(i * size, (i + 1) * size)


def kernel(
    q, k, v, o, g, lse, doc,
    grads,
    Q, K, V, G, LH, L, D, delta, stats, doc_in, lse_in, g_in, o_in,
    qs, ks, vs, gs, kt, probs, lse_s, delta_s,
    dq, dk, dv, pq, rs, rq, rk, rv, res,
    z_send, z_recv, own, d_send, d_recv,
    hub_send, hub_recv, plane_send, plane_recv,
    x_send, x_recv, y_send, y_recv, s_send, s_recv,
    xv_send, xv_recv, p_send, p_recv,
    q_send, q_recv, k_send, k_recv, v_send, v_recv, h_send, h_recv,
):
    x, y, z, c = here()
    plane = x * NY + y
    sib = device(x, y, z, 1 - c)
    hub = z == plane
    scale = DH**-0.5

    barrier = pltpu.get_barrier_semaphore()

    def greet(to):
        pl.semaphore_signal(barrier, inc=1, device_id=to, device_id_type=MESH)

    def plane_peer(i):
        other = lax.rem(plane + i + 1, NX * NY)
        return device(lax.div(other, NY), lax.rem(other, NY), z, c)

    peers(lambda i: greet(device(x, y, ring(z, i, NZ), c)))
    fetch = [
        pltpu.make_async_copy(src, dst, own.at[10 + i])
        for i, (src, dst) in enumerate(((doc, doc_in), (lse, lse_in), (g, g_in), (o, o_in)))
    ]
    for copy in fetch:
        copy.start()
    for i in range(NX - 1):
        greet(device(ring(x, i, NX), y, z, c))
        greet(device(x, ring(y, i, NY), z, c))
    greet(sib)

    @pl.when(hub)
    def _():
        loop(NX * NY - 1, lambda i: greet(plane_peer(i)))

    @pl.when(jnp.logical_not(hub))
    def _():
        greet(device(lax.div(z, NY), lax.rem(z, NY), z, c))

    pl.semaphore_wait(
        barrier, NZ - 1 + NX - 1 + NY - 1 + 1 + jnp.where(hub, NX * NY - 1, 1)
    )

    def lse_copy(frm):
        return remote(stats, LH.at[frm], hub_send, hub_recv.at[frm], device(x, y, plane, c))

    lse_own = pltpu.make_async_copy(stats, LH.at[z], own.at[4])

    srcs = (q, k, g, v)

    def landing(a, zs):
        return (Q.at[zs, c, y], K.at[zs, x], G.at[zs, c, y], V.at[zs, x])[a]

    def z_copy(a, i):
        to = ring(z, i, NZ)
        return remote(
            srcs[a].at[:, columns(to)], landing(a, z), z_send.at[a, slot(i)], z_recv.at[a, z],
            device(x, y, to, c),
        )

    def own_copy(a):
        return pltpu.make_async_copy(srcs[a].at[:, columns(z)], landing(a, z), own.at[a])

    def z_start(a):
        own_copy(a).start()
        peers(lambda i: z_copy(a, i).start())

    def z_wait_from(a, i):
        frm = ring(z, i, NZ)
        remote(
            srcs[a].at[:, columns(frm)], landing(a, frm), z_send.at[a, slot(i)], z_recv.at[a, frm],
            device(x, y, frm, c),
        ).wait_recv()

    def z_wait(a):
        own_copy(a).wait()
        peers(lambda i: z_wait_from(a, i))

    z_start(0)

    lane = lax.broadcasted_iota(jnp.int32, (ROWS, DH), 1)
    fetch[0].wait()
    fetch[1].wait()
    numbers = doc_in[...].reshape(1, CTX_ROWS)
    counts = jnp.zeros((1, DH), F32)
    for d in range(3):
        before = jnp.sum((numbers <= d).astype(F32), axis=1, keepdims=True)
        counts = jnp.where(lane[:1] == d, before, counts)
    for xx in range(NX):
        stats[xx] = jnp.concatenate([lse_in[:, block(xx, PART)], counts[:, : DH - PART]], axis=1)

    @pl.when(hub)
    def _():
        lse_own.start()

    @pl.when(jnp.logical_not(hub))
    def _():
        lse_copy(z).start()

    z_start(1)

    fetch[2].wait()
    fetch[3].wait()
    sums = jnp.zeros((ROWS, DH), F32)
    for h in range(NZ):
        cols = block(h, DH)
        row = jnp.sum(g_in[:, cols].astype(F32) * o_in[:, cols].astype(F32), axis=1, keepdims=True)
        sums = jnp.where(lane == h, row, sums)
    turned = jnp.concatenate([sums, jnp.zeros((DH - ROWS, DH), F32)], axis=0).T
    for h in range(NZ):
        delta[h] = turned[h : h + 1, :]

    def delta_copy(i, to, frm):
        return remote(
            delta.at[to], D.at[frm, c, y], d_send.at[slot(i)], d_recv.at[frm], device(x, y, ring(z, i, NZ), c)
        )

    delta_own = pltpu.make_async_copy(delta.at[z], D.at[z, c, y], own.at[6])
    delta_own.start()
    peers(lambda i: delta_copy(i, ring(z, i, NZ), z).start())
    z_start(2)
    z_start(3)

    def sib_copy(part, slot):
        return remote(part, part, s_send.at[slot], s_recv.at[slot], sib)

    ys = (Q, G, D)

    def y_copy(a, i, frm, to):
        part = ys[a].at[:, c, frm]
        return remote(part, part, y_send.at[a, i], y_recv.at[a, frm], device(x, to, z, c))

    def sib_y(a, frm, core):
        return sib_copy(ys[a].at[:, core, frm], a * NY + frm)

    def y_start(a):
        for i in range(NY - 1):
            y_copy(a, i, y, ring(y, i, NY)).start()
        sib_y(a, y, c).start()

    def y_relay(a):
        for i in range(NY - 1):
            frm = ring(y, i, NY)
            y_copy(a, i, frm, y).wait_recv()
            sib_y(a, frm, c).start()

    def y_wait(a):
        for frm in range(NY):
            sib_y(a, frm, 1 - c).wait_recv()

    def x_copy(i, frm, to):
        part = K.at[:, frm]
        return remote(part, part, x_send.at[i], x_recv.at[frm], device(to, y, z, c))

    def xv_copy(i, zs, frm, to):
        part = V.at[zs, frm]
        return remote(part, part, xv_send.at[i, zs], xv_recv.at[frm, zs], device(to, y, z, c))

    def xv_start(zs):
        for i in range(NX - 1):
            xv_copy(i, zs, x, ring(x, i, NX)).start()

    def pass_values():
        def one(i):
            z_wait_from(3, i)
            xv_start(ring(z, i, NZ))

        peers(one)

    def plane_copy(i):
        other = lax.rem(plane + i + 1, NX * NY)
        return remote(
            LH.at[:, lax.div(other, NY)], L.at[c], plane_send.at[i], plane_recv, plane_peer(i)
        )

    def lse_sib(core):
        return sib_copy(L.at[core], 3 * NY)

    z_wait(0)
    y_start(0)

    @pl.when(hub)
    def _():
        lse_own.wait()

        def one(i):
            lse_copy(ring(z, i, NZ)).wait_recv()

        peers(one)
        loop(NX * NY - 1, lambda i: plane_copy(i).start())
        pltpu.make_async_copy(LH.at[:, x], L.at[c], own.at[5]).start()

    z_wait(1)
    for i in range(NX - 1):
        x_copy(i, x, ring(x, i, NX)).start()

    @pl.when(hub)
    def _():
        pltpu.make_async_copy(LH.at[:, x], L.at[c], own.at[5]).wait()

    @pl.when(jnp.logical_not(hub))
    def _():
        plane_copy(0).wait_recv()

    lse_sib(c).start()
    delta_own.wait()
    peers(lambda i: delta_copy(i, z, ring(z, i, NZ)).wait_recv())
    y_start(2)
    y_relay(0)
    z_wait(2)
    y_start(1)
    lse_sib(1 - c).wait_recv()
    rows = [jnp.concatenate([L[core, zz] for zz in range(NZ)], axis=0) for core in range(NC)]
    counts = rows[0][:, PART:] + rows[1][:, PART:]
    ends = [jnp.sum(counts[:, d : d + 1]).astype(jnp.int32) for d in range(3)]

    def doc_start(pos):
        start = jnp.where(pos >= ends[0], ends[0], 0)
        start = jnp.where(pos >= ends[1], ends[1], start)
        return jnp.where(pos >= ends[2], ends[2], start)

    def lay_rows(by_plane, out):
        for j in range(N_BLK):
            out[j] = jnp.concatenate([by_plane[zz : zz + 1] for zz in range(BLK * j, BLK * (j + 1))], axis=1)

    lay_rows(jnp.concatenate([of_core[:, :PART] for of_core in rows], axis=1), lse_s)

    q_at = lax.broadcasted_iota(jnp.int32, (1, Q_BLK), 1)
    q_in = lax.rem(q_at, Q_Z)
    q_base = (
        lax.div(q_at, Q_Z) * SPAN + lax.div(q_in, PART) * CTX_ROWS + x * PART + lax.rem(q_in, PART)
    )
    k_at = lax.broadcasted_iota(jnp.int32, (K_BLK, 1), 0)
    k_in = lax.rem(k_at, K_Z)
    k_base = (
        lax.div(k_at, K_Z) * SPAN
        + c * CTX_ROWS
        + lax.div(k_in, ROWS) * PART
        + y * ROWS
        + lax.rem(k_in, ROWS)
    )

    def flat(src, out, rows):
        def step(zz):
            at = pl.ds(pl.multiple_of(zz * rows, rows), rows)
            out[at, :] = src[zz].astype(F32).reshape(rows, DH).astype(BF16)

        loop(NZ, step)

    y_wait(0)
    flat(Q, qs, Q_Z)
    for i in range(NX - 1):
        x_copy(i, ring(x, i, NX), x).wait_recv()
    flat(K, ks, K_Z)

    def probs_block(j):
        q_pos = q_base + j * (BLK * SPAN)
        start = doc_start(q_pos)
        for i in range(j + 1):
            k_pos = k_base + i * (BLK * SPAN)
            allowed = jnp.where(k_pos < ends[0], NZ * SPAN, k_pos) >= start
            if i == j:
                allowed = allowed & (k_pos <= q_pos)
            s = contract_last(ks[block(i, K_BLK), :], qs[block(j, Q_BLK), :])
            p = jnp.where(allowed, jnp.exp(s * scale - lse_s[j]), 0.0)
            probs[block(i, K_BLK), block(j, Q_BLK)] = p.astype(BF16)

    probs_block(0)
    probs_block(1)
    own_copy(3).wait()
    xv_start(z)
    pass_values()
    probs_block(2)
    y_relay(1)
    probs_block(3)
    y_relay(2)

    y_wait(1)
    flat(G, gs, Q_Z)

    def v_copy(i, frm, to):
        return remote(dv.at[:, to], rv.at[frm], v_send.at[i], v_recv.at[frm], device(to, y, z, c))

    for i in range(N_BLK):
        total = jnp.dot(
            probs[block(i, K_BLK), i * Q_BLK :], gs[i * Q_BLK :, :], preferred_element_type=F32
        )
        dv[BLK * i : BLK * (i + 1)] = total.reshape(BLK, NX, ROWS, DH).astype(BF16)
    for i in range(NX - 1):
        v_copy(i, x, ring(x, i, NX)).start()

    y_wait(2)
    parts = []
    for core in range(NC):
        for yy in range(NY):
            parts.append(jnp.concatenate([D[zz, core, yy] for zz in range(NZ)], axis=0)[:, :ROWS])
    lay_rows(jnp.concatenate(parts, axis=1), delta_s)
    for i in range(N_BLK):
        kt[i] = ks[block(i, K_BLK), :].T
    for i in range(NX - 1):
        loop(NZ, lambda zs, i=i: xv_copy(i, zs, ring(x, i, NX), x).wait_recv())
    flat(V, vs, K_Z)

    def k_copy(j, i, frm, to):
        rows = pl.ds(BLK * j, BLK)
        return remote(
            dk.at[rows, to], rk.at[frm, rows], k_send.at[j, i], k_recv.at[j, frm], device(to, y, z, c)
        )

    def p_copy(j, core):
        rows = pl.ds(BLK * j, BLK)
        return remote(dq.at[rows, core], rs.at[rows], p_send.at[j], p_recv.at[j], sib)

    def q_copy(j, i, frm, to):
        rows = pl.ds(BLK * j, BLK)
        return remote(
            pq.at[rows, to], rq.at[frm, rows], q_send.at[j, i], q_recv.at[j, frm], device(x, to, z, c)
        )

    def grads_block(j):
        total = jnp.zeros((DH, Q_BLK), F32)
        for i in range(j + 1):
            dp = contract_last(vs[block(i, K_BLK), :], gs[block(j, Q_BLK), :])
            p = probs[block(i, K_BLK), block(j, Q_BLK)].astype(F32)
            ds = (p * (dp - delta_s[j])).astype(BF16)
            probs[block(i, K_BLK), block(j, Q_BLK)] = ds
            total += jnp.dot(kt[i], ds, preferred_element_type=F32)
        dq[BLK * j : BLK * (j + 1)] = total.T.reshape(BLK, NC, NY, ROWS, DH).astype(BF16)
        p_copy(j, 1 - c).start()
        total = jnp.dot(
            probs[block(j, K_BLK), j * Q_BLK :], qs[j * Q_BLK :, :], preferred_element_type=F32
        )
        dk[BLK * j : BLK * (j + 1)] = total.reshape(BLK, NX, ROWS, DH).astype(BF16)
        for i in range(NX - 1):
            k_copy(j, i, x, ring(x, i, NX)).start()

    parts_of = (pl.ds(0, 2), pl.ds(2, 1))

    def home_copy(a, to, frm):
        return remote(
            res.at[parts_of[a], to], grads.at[parts_of[a], :, columns(frm)],
            h_send.at[a, to], h_recv.at[a, frm], device(x, y, to, c),
        )

    def home_own(a):
        return pltpu.make_async_copy(
            res.at[parts_of[a], z], grads.at[parts_of[a], :, columns(z)], own.at[7 + a]
        )

    def send_home(a, to):
        @pl.when(to == z)
        def _():
            home_own(a).start()

        @pl.when(to != z)
        def _():
            home_copy(a, to, z).start()

    def add_v():
        for i in range(NX - 1):
            v_copy(i, ring(x, i, NX), x).wait_recv()

        def one(zz):
            total = dv[zz, x].astype(F32)
            for i in range(NX - 1):
                total += rv[ring(x, i, NX), zz].astype(F32)
            res[2, zz] = total.astype(BF16)

        loop(NZ, one)
        home_own(1).start()
        peers(lambda i: home_copy(1, ring(z, i, NZ), z).start())

    def pair_block(j):
        p_copy(j, c).wait_recv()

        def one(step):
            zz = BLK * j + step
            pq[zz] = (dq[zz, c].astype(F32) + rs[zz].astype(F32)).astype(BF16)

        loop(BLK, one)
        for i in range(NY - 1):
            q_copy(j, i, y, ring(y, i, NY)).start()

    def add_block(j):
        for i in range(NX - 1):
            k_copy(j, i, ring(x, i, NX), x).wait_recv()
        for i in range(NY - 1):
            q_copy(j, i, ring(y, i, NY), y).wait_recv()

        def one(step):
            zz = BLK * j + step
            total = dk[zz, x].astype(F32)
            for i in range(NX - 1):
                total += rk[ring(x, i, NX), zz].astype(F32)
            res[1, zz] = (total * scale).astype(BF16)
            total = pq[zz, y].astype(F32)
            for i in range(NY - 1):
                total += rq[ring(y, i, NY), zz].astype(F32)
            res[0, zz] = (total * scale).astype(BF16)
            send_home(0, zz)

        loop(BLK, one)

    grads_block(3)
    grads_block(2)
    pair_block(3)
    grads_block(1)
    pair_block(2)
    add_v()
    grads_block(0)
    pair_block(1)
    pair_block(0)
    add_block(3)
    add_block(2)
    add_block(1)
    add_block(0)

    for a in range(4):
        peers(lambda i, a=a: z_copy(a, i).wait_send())
    peers(lambda i: delta_copy(i, ring(z, i, NZ), z).wait_send())

    @pl.when(jnp.logical_not(hub))
    def _():
        lse_copy(z).wait_send()

    @pl.when(hub)
    def _():
        loop(NX * NY - 1, lambda i: plane_copy(i).wait_send())

    for i in range(NX - 1):
        x_copy(i, x, ring(x, i, NX)).wait_send()
        loop(NZ, lambda zs, i=i: xv_copy(i, zs, x, ring(x, i, NX)).wait_send())
    for a in range(3):
        for i in range(NY - 1):
            y_copy(a, i, y, ring(y, i, NY)).wait_send()
        for frm in range(NY):
            sib_y(a, frm, c).wait_send()
    lse_sib(c).wait_send()
    for i in range(NX - 1):
        v_copy(i, x, ring(x, i, NX)).wait_send()
    for j in range(N_BLK):
        for i in range(NX - 1):
            k_copy(j, i, x, ring(x, i, NX)).wait_send()
        for i in range(NY - 1):
            q_copy(j, i, y, ring(y, i, NY)).wait_send()
        p_copy(j, 1 - c).wait_send()
    for a in (1, 0):
        home_own(a).wait()

        def one(i, a=a):
            peer = ring(z, i, NZ)
            home_copy(a, peer, z).wait_send()
            home_copy(a, z, peer).wait_recv()

        peers(one)


def copy_kernel(grads, out_q, out_k, out_v):
    for i, out in enumerate((out_q, out_k, out_v)):
        out[...] = grads[i]


def copied(grads):
    vmem = pl.BlockSpec(memory_space=pltpu.VMEM)
    out = jax.ShapeDtypeStruct((ROWS, NZ * DH), BF16)
    return pl.pallas_call(
        copy_kernel, out_shape=(out,) * 3, in_specs=[vmem], out_specs=(vmem,) * 3, name="copy_grads"
    )(grads)


def per_device(queries, keys, values, outputs, grad_out, log_sums, doc_ids):
    dma = pltpu.SemaphoreType.DMA
    hbm = pl.BlockSpec(memory_space=pl.ANY)
    kv, qg = (NZ, NX, ROWS, DH), (NZ, NC, NY, ROWS, DH)
    grads = pl.pallas_call(
        kernel,
        out_shape=jax.ShapeDtypeStruct((3, ROWS, NZ * DH), BF16),
        in_specs=[pl.BlockSpec(memory_space=pltpu.HBM)] * 7,
        out_specs=hbm,
        scratch_shapes=[
            pltpu.VMEM(qg, BF16), pltpu.VMEM(kv, BF16), pltpu.VMEM(kv, BF16), pltpu.VMEM(qg, BF16),
            pltpu.VMEM((NZ, NX, 1, DH), F32), pltpu.VMEM((NC, NZ, 1, DH), F32),
            pltpu.VMEM((NZ, NC, NY, 1, DH), F32),
            pltpu.VMEM((NZ, 1, DH), F32), pltpu.VMEM((NX, 1, DH), F32),
            pltpu.VMEM((CTX_ROWS,), jnp.int32), pltpu.VMEM((1, CTX_ROWS), F32), pltpu.VMEM((ROWS, NZ * DH), BF16), pltpu.VMEM((ROWS, NZ * DH), BF16),
            pltpu.VMEM((NZ * Q_Z, DH), BF16), pltpu.VMEM((NZ * K_Z, DH), BF16),
            pltpu.VMEM((NZ * K_Z, DH), BF16), pltpu.VMEM((NZ * Q_Z, DH), BF16),
            pltpu.VMEM((N_BLK, DH, K_BLK), BF16), pltpu.VMEM((NZ * K_Z, NZ * Q_Z), BF16),
            pltpu.VMEM((N_BLK, 1, Q_BLK), F32), pltpu.VMEM((N_BLK, 1, Q_BLK), F32),
            pltpu.VMEM(qg, BF16), pltpu.VMEM(kv, BF16), pltpu.VMEM(kv, BF16),
            pltpu.VMEM((NZ, NY, ROWS, DH), BF16), pltpu.VMEM((NZ, NY, ROWS, DH), BF16),
            pltpu.VMEM((NY, NZ, ROWS, DH), BF16),
            pltpu.VMEM((NX, NZ, ROWS, DH), BF16), pltpu.VMEM((NX, NZ, ROWS, DH), BF16),
            pltpu.VMEM((3, NZ, ROWS, DH), BF16),
            dma((4, NZ - 1)), dma((4, NZ)), dma((14,)),
            dma((NZ - 1,)), dma((NZ,)),
            dma, dma((NZ,)), dma((NX * NY - 1,)), dma,
            dma((NX - 1,)), dma((NX,)), dma((3, NY - 1)), dma((3, NY)),
            dma((3 * NY + 1,)), dma((3 * NY + 1,)),
            dma((NX - 1, NZ)), dma((NX, NZ)), dma((N_BLK,)), dma((N_BLK,)),
            dma((N_BLK, NY - 1)), dma((N_BLK, NY)), dma((N_BLK, NX - 1)), dma((N_BLK, NX)),
            dma((NX - 1,)), dma((NX,)), dma((2, NZ)), dma((2, NZ)),
        ],
        compiler_params=pltpu.CompilerParams(
            collective_id=0, has_side_effects=True, vmem_limit_bytes=60 * 1024 * 1024
        ),
        name="attention_grads",
    )(queries, keys, values, outputs, grad_out, log_sums, doc_ids)
    return copied(grads)


def solution(mesh):
    tokens = P(("ctx", "head"), None)
    return jax.shard_map(
        per_device,
        mesh=mesh,
        in_specs=(tokens,) * 5 + (P("head", "ctx"), P("ctx")),
        out_specs=(tokens,) * 3,
        check_vma=False,
    )
```

```python
import jax
import jax.numpy as jnp
from jax import lax
from jax.experimental import pallas as pl
from jax.experimental.pallas import tpu as pltpu
from jax.sharding import PartitionSpec as P

DH = 128
NX, NY, NZ, NC = 4, 4, 16, 2
ROWS = 24
CTX_ROWS = NX * NY * ROWS
SPAN = NC * CTX_ROWS
Q_Z = NC * NY * ROWS
K_Z = NX * ROWS
BLK = 4
N_BLK = NZ // BLK
Q_BLK = BLK * Q_Z
K_BLK = BLK * K_Z
PART = NY * ROWS
MESH = pl.DeviceIdType.MESH
F32 = jnp.float32
BF16 = jnp.bfloat16


def here():
    ctx, head = lax.axis_index("ctx"), lax.axis_index("head")
    return lax.div(head, NY), lax.rem(head, NY), lax.div(ctx, NC), lax.rem(ctx, NC)


def device(x, y, z, c):
    return (z * NC + c, x * NY + y)


def ring(me, step, size):
    away, up = step if isinstance(step, tuple) else (step // 2 + 1, step % 2 == 0)
    if up:
        return jnp.where(me + away >= size, me + away - size, me + away)
    return jnp.where(me < away, me - away + size, me - away)


def slot(step):
    away, up = step
    return 2 * (away - 1) + (0 if up else 1)


def peers(body):
    def step(i, carry):
        body((NZ // 2 - 1 - i, True))
        body((NZ // 2 - 1 - i, False))
        return carry

    body((NZ // 2, True))
    lax.fori_loop(0, NZ // 2 - 1, step, 0)


def columns(head):
    return pl.ds(pl.multiple_of(head * DH, DH), DH)


def remote(src, dst, send, recv, to):
    return pltpu.make_async_remote_copy(
        src_ref=src, dst_ref=dst, send_sem=send, recv_sem=recv, device_id=to, device_id_type=MESH
    )


def loop(count, body):
    def step(i, carry):
        body(i)
        return carry

    lax.fori_loop(0, count, step, 0)


def contract_last(left, right):
    return lax.dot_general(left, right, (((1,), (1,)), ((), ())), preferred_element_type=F32)


def block(i, size):
    return slice(i * size, (i + 1) * size)


def kernel(
    q, k, v, o, g, lse, doc,
    grads,
    Q, K, V, G, LH, L, D, delta, stats, doc_in, lse_in, g_in, o_in,
    qs, ks, vs, gs, kt, probs, lse_s, delta_s,
    dq, dk, dv, pq, rs, rq, rk, rv, res,
    z_send, z_recv, own, d_send, d_recv,
    hub_send, hub_recv, plane_send, plane_recv,
    x_send, x_recv, y_send, y_recv, s_send, s_recv,
    xv_send, xv_recv, p_send, p_recv,
    q_send, q_recv, k_send, k_recv, v_send, v_recv, h_send, h_recv,
):
    x, y, z, c = here()
    plane = x * NY + y
    sib = device(x, y, z, 1 - c)
    hub = z == plane
    scale = DH**-0.5

    barrier = pltpu.get_barrier_semaphore()

    def greet(to):
        pl.semaphore_signal(barrier, inc=1, device_id=to, device_id_type=MESH)

    def plane_peer(i):
        other = lax.rem(plane + i + 1, NX * NY)
        return device(lax.div(other, NY), lax.rem(other, NY), z, c)

    peers(lambda i: greet(device(x, y, ring(z, i, NZ), c)))
    fetch = [
        pltpu.make_async_copy(src, dst, own.at[10 + i])
        for i, (src, dst) in enumerate(((doc, doc_in), (lse, lse_in), (g, g_in), (o, o_in)))
    ]
    for copy in fetch:
        copy.start()
    for i in range(NX - 1):
        greet(device(ring(x, i, NX), y, z, c))
        greet(device(x, ring(y, i, NY), z, c))
    greet(sib)

    @pl.when(hub)
    def _():
        loop(NX * NY - 1, lambda i: greet(plane_peer(i)))

    @pl.when(jnp.logical_not(hub))
    def _():
        greet(device(lax.div(z, NY), lax.rem(z, NY), z, c))

    pl.semaphore_wait(
        barrier, NZ - 1 + NX - 1 + NY - 1 + 1 + jnp.where(hub, NX * NY - 1, 1)
    )

    def lse_copy(frm):
        return remote(stats, LH.at[frm], hub_send, hub_recv.at[frm], device(x, y, plane, c))

    lse_own = pltpu.make_async_copy(stats, LH.at[z], own.at[4])

    srcs = (q, k, g, v)

    def landing(a, zs):
        return (Q.at[zs, c, y], K.at[zs, x], G.at[zs, c, y], V.at[zs, x])[a]

    def z_copy(a, i):
        to = ring(z, i, NZ)
        return remote(
            srcs[a].at[:, columns(to)], landing(a, z), z_send.at[a, slot(i)], z_recv.at[a, z],
            device(x, y, to, c),
        )

    def own_copy(a):
        return pltpu.make_async_copy(srcs[a].at[:, columns(z)], landing(a, z), own.at[a])

    def z_start(a):
        own_copy(a).start()
        peers(lambda i: z_copy(a, i).start())

    def z_wait_from(a, i):
        frm = ring(z, i, NZ)
        remote(
            srcs[a].at[:, columns(frm)], landing(a, frm), z_send.at[a, slot(i)], z_recv.at[a, frm],
            device(x, y, frm, c),
        ).wait_recv()

    def z_wait(a):
        own_copy(a).wait()
        peers(lambda i: z_wait_from(a, i))

    z_start(0)

    lane = lax.broadcasted_iota(jnp.int32, (ROWS, DH), 1)
    fetch[0].wait()
    fetch[1].wait()
    numbers = doc_in[...].reshape(1, CTX_ROWS)
    counts = jnp.zeros((1, DH), F32)
    for d in range(3):
        before = jnp.sum((numbers <= d).astype(F32), axis=1, keepdims=True)
        counts = jnp.where(lane[:1] == d, before, counts)
    for xx in range(NX):
        stats[xx] = jnp.concatenate([lse_in[:, block(xx, PART)], counts[:, : DH - PART]], axis=1)

    @pl.when(hub)
    def _():
        lse_own.start()

    @pl.when(jnp.logical_not(hub))
    def _():
        lse_copy(z).start()

    z_start(1)

    fetch[2].wait()
    fetch[3].wait()
    sums = jnp.zeros((ROWS, DH), F32)
    for h in range(NZ):
        cols = block(h, DH)
        row = jnp.sum(g_in[:, cols].astype(F32) * o_in[:, cols].astype(F32), axis=1, keepdims=True)
        sums = jnp.where(lane == h, row, sums)
    turned = jnp.concatenate([sums, jnp.zeros((DH - ROWS, DH), F32)], axis=0).T
    for h in range(NZ):
        delta[h] = turned[h : h + 1, :]

    def delta_copy(i, to, frm):
        return remote(
            delta.at[to], D.at[frm, c, y], d_send.at[slot(i)], d_recv.at[frm], device(x, y, ring(z, i, NZ), c)
        )

    delta_own = pltpu.make_async_copy(delta.at[z], D.at[z, c, y], own.at[6])
    delta_own.start()
    peers(lambda i: delta_copy(i, ring(z, i, NZ), z).start())
    z_start(2)
    z_start(3)

    def sib_copy(part, slot):
        return remote(part, part, s_send.at[slot], s_recv.at[slot], sib)

    ys = (Q, G, D)

    def y_copy(a, i, frm, to):
        part = ys[a].at[:, c, frm]
        return remote(part, part, y_send.at[a, i], y_recv.at[a, frm], device(x, to, z, c))

    def sib_y(a, frm, core):
        return sib_copy(ys[a].at[:, core, frm], a * NY + frm)

    def y_start(a):
        for i in range(NY - 1):
            y_copy(a, i, y, ring(y, i, NY)).start()
        sib_y(a, y, c).start()

    def y_relay(a):
        for i in range(NY - 1):
            frm = ring(y, i, NY)
            y_copy(a, i, frm, y).wait_recv()
            sib_y(a, frm, c).start()

    def y_wait(a):
        for frm in range(NY):
            sib_y(a, frm, 1 - c).wait_recv()

    def x_copy(i, frm, to):
        part = K.at[:, frm]
        return remote(part, part, x_send.at[i], x_recv.at[frm], device(to, y, z, c))

    def xv_copy(i, zs, frm, to):
        part = V.at[zs, frm]
        return remote(part, part, xv_send.at[i, zs], xv_recv.at[frm, zs], device(to, y, z, c))

    def xv_start(zs):
        for i in range(NX - 1):
            xv_copy(i, zs, x, ring(x, i, NX)).start()

    def pass_values():
        def one(i):
            z_wait_from(3, i)
            xv_start(ring(z, i, NZ))

        peers(one)

    def plane_copy(i):
        other = lax.rem(plane + i + 1, NX * NY)
        return remote(
            LH.at[:, lax.div(other, NY)], L.at[c], plane_send.at[i], plane_recv, plane_peer(i)
        )

    def lse_sib(core):
        return sib_copy(L.at[core], 3 * NY)

    z_wait(0)
    y_start(0)

    @pl.when(hub)
    def _():
        lse_own.wait()

        def one(i):
            lse_copy(ring(z, i, NZ)).wait_recv()

        peers(one)
        loop(NX * NY - 1, lambda i: plane_copy(i).start())
        pltpu.make_async_copy(LH.at[:, x], L.at[c], own.at[5]).start()

    z_wait(1)
    for i in range(NX - 1):
        x_copy(i, x, ring(x, i, NX)).start()

    @pl.when(hub)
    def _():
        pltpu.make_async_copy(LH.at[:, x], L.at[c], own.at[5]).wait()

    @pl.when(jnp.logical_not(hub))
    def _():
        plane_copy(0).wait_recv()

    lse_sib(c).start()
    delta_own.wait()
    peers(lambda i: delta_copy(i, z, ring(z, i, NZ)).wait_recv())
    y_start(2)
    y_relay(0)
    z_wait(2)
    y_start(1)
    lse_sib(1 - c).wait_recv()
    rows = [jnp.concatenate([L[core, zz] for zz in range(NZ)], axis=0) for core in range(NC)]
    counts = rows[0][:, PART:] + rows[1][:, PART:]
    ends = [jnp.sum(counts[:, d : d + 1]).astype(jnp.int32) for d in range(3)]

    def doc_start(pos):
        start = jnp.where(pos >= ends[0], ends[0], 0)
        start = jnp.where(pos >= ends[1], ends[1], start)
        return jnp.where(pos >= ends[2], ends[2], start)

    def lay_rows(by_plane, out):
        for j in range(N_BLK):
            out[j] = jnp.concatenate([by_plane[zz : zz + 1] for zz in range(BLK * j, BLK * (j + 1))], axis=1)

    lay_rows(jnp.concatenate([of_core[:, :PART] for of_core in rows], axis=1), lse_s)

    q_at = lax.broadcasted_iota(jnp.int32, (1, Q_BLK), 1)
    q_in = lax.rem(q_at, Q_Z)
    q_base = (
        lax.div(q_at, Q_Z) * SPAN + lax.div(q_in, PART) * CTX_ROWS + x * PART + lax.rem(q_in, PART)
    )
    k_at = lax.broadcasted_iota(jnp.int32, (K_BLK, 1), 0)
    k_in = lax.rem(k_at, K_Z)
    k_base = (
        lax.div(k_at, K_Z) * SPAN
        + c * CTX_ROWS
        + lax.div(k_in, ROWS) * PART
        + y * ROWS
        + lax.rem(k_in, ROWS)
    )

    def flat(src, out, rows):
        def step(zz):
            at = pl.ds(pl.multiple_of(zz * rows, rows), rows)
            out[at, :] = src[zz].astype(F32).reshape(rows, DH).astype(BF16)

        loop(NZ, step)

    y_wait(0)
    flat(Q, qs, Q_Z)
    for i in range(NX - 1):
        x_copy(i, ring(x, i, NX), x).wait_recv()
    flat(K, ks, K_Z)

    def probs_block(j):
        q_pos = q_base + j * (BLK * SPAN)
        start = doc_start(q_pos)
        for i in range(j + 1):
            k_pos = k_base + i * (BLK * SPAN)
            allowed = jnp.where(k_pos < ends[0], NZ * SPAN, k_pos) >= start
            if i == j:
                allowed = allowed & (k_pos <= q_pos)
            s = contract_last(ks[block(i, K_BLK), :], qs[block(j, Q_BLK), :])
            p = jnp.where(allowed, jnp.exp(s * scale - lse_s[j]), 0.0)
            probs[block(i, K_BLK), block(j, Q_BLK)] = p.astype(BF16)

    probs_block(0)
    probs_block(1)
    own_copy(3).wait()
    xv_start(z)
    pass_values()
    probs_block(2)
    y_relay(1)
    probs_block(3)
    y_relay(2)

    y_wait(1)
    flat(G, gs, Q_Z)

    def v_copy(i, frm, to):
        return remote(dv.at[:, to], rv.at[frm], v_send.at[i], v_recv.at[frm], device(to, y, z, c))

    for i in range(N_BLK):
        total = jnp.dot(
            probs[block(i, K_BLK), i * Q_BLK :], gs[i * Q_BLK :, :], preferred_element_type=F32
        )
        dv[BLK * i : BLK * (i + 1)] = total.reshape(BLK, NX, ROWS, DH).astype(BF16)
    for i in range(NX - 1):
        v_copy(i, x, ring(x, i, NX)).start()

    y_wait(2)
    parts = []
    for core in range(NC):
        for yy in range(NY):
            parts.append(jnp.concatenate([D[zz, core, yy] for zz in range(NZ)], axis=0)[:, :ROWS])
    lay_rows(jnp.concatenate(parts, axis=1), delta_s)
    for i in range(N_BLK):
        kt[i] = ks[block(i, K_BLK), :].T
    for i in range(NX - 1):
        loop(NZ, lambda zs, i=i: xv_copy(i, zs, ring(x, i, NX), x).wait_recv())
    flat(V, vs, K_Z)

    def k_copy(j, i, frm, to):
        rows = pl.ds(BLK * j, BLK)
        return remote(
            dk.at[rows, to], rk.at[frm, rows], k_send.at[j, i], k_recv.at[j, frm], device(to, y, z, c)
        )

    def p_copy(j, core):
        rows = pl.ds(BLK * j, BLK)
        return remote(dq.at[rows, core], rs.at[rows], p_send.at[j], p_recv.at[j], sib)

    def q_copy(j, i, frm, to):
        rows = pl.ds(BLK * j, BLK)
        return remote(
            pq.at[rows, to], rq.at[frm, rows], q_send.at[j, i], q_recv.at[j, frm], device(x, to, z, c)
        )

    def grads_block(j):
        total = jnp.zeros((DH, Q_BLK), F32)
        for i in range(j + 1):
            dp = contract_last(vs[block(i, K_BLK), :], gs[block(j, Q_BLK), :])
            p = probs[block(i, K_BLK), block(j, Q_BLK)].astype(F32)
            ds = (p * (dp - delta_s[j])).astype(BF16)
            probs[block(i, K_BLK), block(j, Q_BLK)] = ds
            total += jnp.dot(kt[i], ds, preferred_element_type=F32)
        dq[BLK * j : BLK * (j + 1)] = total.T.reshape(BLK, NC, NY, ROWS, DH).astype(BF16)
        p_copy(j, 1 - c).start()
        total = jnp.dot(
            probs[block(j, K_BLK), j * Q_BLK :], qs[j * Q_BLK :, :], preferred_element_type=F32
        )
        dk[BLK * j : BLK * (j + 1)] = total.reshape(BLK, NX, ROWS, DH).astype(BF16)
        for i in range(NX - 1):
            k_copy(j, i, x, ring(x, i, NX)).start()

    parts_of = (pl.ds(0, 2), pl.ds(2, 1))

    def home_copy(a, to, frm):
        return remote(
            res.at[parts_of[a], to], grads.at[parts_of[a], :, columns(frm)],
            h_send.at[a, to], h_recv.at[a, frm], device(x, y, to, c),
        )

    def home_own(a):
        return pltpu.make_async_copy(
            res.at[parts_of[a], z], grads.at[parts_of[a], :, columns(z)], own.at[7 + a]
        )

    def send_home(a, to):
        @pl.when(to == z)
        def _():
            home_own(a).start()

        @pl.when(to != z)
        def _():
            home_copy(a, to, z).start()

    def add_v():
        for i in range(NX - 1):
            v_copy(i, ring(x, i, NX), x).wait_recv()

        def one(zz):
            total = dv[zz, x].astype(F32)
            for i in range(NX - 1):
                total += rv[ring(x, i, NX), zz].astype(F32)
            res[2, zz] = total.astype(BF16)

        loop(NZ, one)
        home_own(1).start()
        peers(lambda i: home_copy(1, ring(z, i, NZ), z).start())

    def pair_block(j):
        p_copy(j, c).wait_recv()

        def one(step):
            zz = BLK * j + step
            pq[zz] = (dq[zz, c].astype(F32) + rs[zz].astype(F32)).astype(BF16)

        loop(BLK, one)
        for i in range(NY - 1):
            q_copy(j, i, y, ring(y, i, NY)).start()

    def add_block(j):
        for i in range(NX - 1):
            k_copy(j, i, ring(x, i, NX), x).wait_recv()
        for i in range(NY - 1):
            q_copy(j, i, ring(y, i, NY), y).wait_recv()

        def one(step):
            zz = BLK * j + step
            total = dk[zz, x].astype(F32)
            for i in range(NX - 1):
                total += rk[ring(x, i, NX), zz].astype(F32)
            res[1, zz] = (total * scale).astype(BF16)
            total = pq[zz, y].astype(F32)
            for i in range(NY - 1):
                total += rq[ring(y, i, NY), zz].astype(F32)
            res[0, zz] = (total * scale).astype(BF16)
            send_home(0, zz)

        loop(BLK, one)

    grads_block(3)
    grads_block(2)
    pair_block(3)
    grads_block(1)
    pair_block(2)
    add_v()
    grads_block(0)
    pair_block(1)
    pair_block(0)
    add_block(3)
    add_block(2)
    add_block(1)
    add_block(0)

    for a in range(4):
        peers(lambda i, a=a: z_copy(a, i).wait_send())
    peers(lambda i: delta_copy(i, ring(z, i, NZ), z).wait_send())

    @pl.when(jnp.logical_not(hub))
    def _():
        lse_copy(z).wait_send()

    @pl.when(hub)
    def _():
        loop(NX * NY - 1, lambda i: plane_copy(i).wait_send())

    for i in range(NX - 1):
        x_copy(i, x, ring(x, i, NX)).wait_send()
        loop(NZ, lambda zs, i=i: xv_copy(i, zs, x, ring(x, i, NX)).wait_send())
    for a in range(3):
        for i in range(NY - 1):
            y_copy(a, i, y, ring(y, i, NY)).wait_send()
        for frm in range(NY):
            sib_y(a, frm, c).wait_send()
    lse_sib(c).wait_send()
    for i in range(NX - 1):
        v_copy(i, x, ring(x, i, NX)).wait_send()
    for j in range(N_BLK):
        for i in range(NX - 1):
            k_copy(j, i, x, ring(x, i, NX)).wait_send()
        for i in range(NY - 1):
            q_copy(j, i, y, ring(y, i, NY)).wait_send()
        p_copy(j, 1 - c).wait_send()
    for a in (1, 0):
        home_own(a).wait()

        def one(i, a=a):
            peer = ring(z, i, NZ)
            home_copy(a, peer, z).wait_send()
            home_copy(a, z, peer).wait_recv()

        peers(one)


def copy_kernel(grads, out_q, out_k, out_v):
    for i, out in enumerate((out_q, out_k, out_v)):
        out[...] = grads[i]


def copied(grads):
    vmem = pl.BlockSpec(memory_space=pltpu.VMEM)
    out = jax.ShapeDtypeStruct((ROWS, NZ * DH), BF16)
    return pl.pallas_call(
        copy_kernel, out_shape=(out,) * 3, in_specs=[vmem], out_specs=(vmem,) * 3, name="copy_grads"
    )(grads)


def per_device(queries, keys, values, outputs, grad_out, log_sums, doc_ids):
    dma = pltpu.SemaphoreType.DMA
    hbm = pl.BlockSpec(memory_space=pl.ANY)
    kv, qg = (NZ, NX, ROWS, DH), (NZ, NC, NY, ROWS, DH)
    grads = pl.pallas_call(
        kernel,
        out_shape=jax.ShapeDtypeStruct((3, ROWS, NZ * DH), BF16),
        in_specs=[pl.BlockSpec(memory_space=pltpu.HBM)] * 7,
        out_specs=hbm,
        scratch_shapes=[
            pltpu.VMEM(qg, BF16), pltpu.VMEM(kv, BF16), pltpu.VMEM(kv, BF16), pltpu.VMEM(qg, BF16),
            pltpu.VMEM((NZ, NX, 1, DH), F32), pltpu.VMEM((NC, NZ, 1, DH), F32),
            pltpu.VMEM((NZ, NC, NY, 1, DH), F32),
            pltpu.VMEM((NZ, 1, DH), F32), pltpu.VMEM((NX, 1, DH), F32),
            pltpu.VMEM((CTX_ROWS,), jnp.int32), pltpu.VMEM((1, CTX_ROWS), F32), pltpu.VMEM((ROWS, NZ * DH), BF16), pltpu.VMEM((ROWS, NZ * DH), BF16),
            pltpu.VMEM((NZ * Q_Z, DH), BF16), pltpu.VMEM((NZ * K_Z, DH), BF16),
            pltpu.VMEM((NZ * K_Z, DH), BF16), pltpu.VMEM((NZ * Q_Z, DH), BF16),
            pltpu.VMEM((N_BLK, DH, K_BLK), BF16), pltpu.VMEM((NZ * K_Z, NZ * Q_Z), BF16),
            pltpu.VMEM((N_BLK, 1, Q_BLK), F32), pltpu.VMEM((N_BLK, 1, Q_BLK), F32),
            pltpu.VMEM(qg, BF16), pltpu.VMEM(kv, BF16), pltpu.VMEM(kv, BF16),
            pltpu.VMEM((NZ, NY, ROWS, DH), BF16), pltpu.VMEM((NZ, NY, ROWS, DH), BF16),
            pltpu.VMEM((NY, NZ, ROWS, DH), BF16),
            pltpu.VMEM((NX, NZ, ROWS, DH), BF16), pltpu.VMEM((NX, NZ, ROWS, DH), BF16),
            pltpu.VMEM((3, NZ, ROWS, DH), BF16),
            dma((4, NZ - 1)), dma((4, NZ)), dma((14,)),
            dma((NZ - 1,)), dma((NZ,)),
            dma, dma((NZ,)), dma((NX * NY - 1,)), dma,
            dma((NX - 1,)), dma((NX,)), dma((3, NY - 1)), dma((3, NY)),
            dma((3 * NY + 1,)), dma((3 * NY + 1,)),
            dma((NX - 1, NZ)), dma((NX, NZ)), dma((N_BLK,)), dma((N_BLK,)),
            dma((N_BLK, NY - 1)), dma((N_BLK, NY)), dma((N_BLK, NX - 1)), dma((N_BLK, NX)),
            dma((NX - 1,)), dma((NX,)), dma((2, NZ)), dma((2, NZ)),
        ],
        compiler_params=pltpu.CompilerParams(
            collective_id=0, has_side_effects=True, vmem_limit_bytes=60 * 1024 * 1024
        ),
        name="attention_grads",
    )(queries, keys, values, outputs, grad_out, log_sums, doc_ids)
    return copied(grads)


def solution(mesh):
    tokens = P(("ctx", "head"), None)
    return jax.shard_map(
        per_device,
        mesh=mesh,
        in_specs=(tokens,) * 5 + (P("head", "ctx"), P("ctx")),
        out_specs=(tokens,) * 3,
        check_vma=False,
    )
```
